32 devices in a mesh: seq: 8 (over z, y), head: 2 (over x), dp: 2 (over core).
Axes of the slice: x: 2, y: 2, z: 4, core: 2. Of those that a mesh axis runs over, the one named last changes fastest.
Arguments:
- inputs: bfloat16 [2, 4096, 3584], P('dp', 'seq', 'head'), may hold values from -6 to 6
- value_weight: bfloat16 [3584, 3584], P(None, 'head'), may hold values from -0.09375 to 0.09375
- cotangent: bfloat16 [2, 4096, 3584], P('dp', 'seq', 'head'), may hold values from -6 to 6
- spikes_q: int32 [2, 4096, 3584], P('dp', 'seq', 'head'), may hold values from 0 to 3
- spikes_k: int32 [2, 4096, 3584], P('dp', 'seq', 'head'), may hold values from 0 to 3
- log_decay: float32 [2, 28, 4096], P('dp', 'head', 'seq'), may hold values from -1.0976562 to 0, as said below
Outputs:
- grad_input: bfloat16 [2, 4096, 3584], P('dp', 'seq', 'head')
- grad_weight: float32 [3584, 3584], P(('seq', 'dp'), 'head')
The draws below stay inside these ranges and needn't reach their ends.
Inputs may be any that keep to these rules, and one draw needn't show every extreme that they name: `spikes_q`: spike count of a token in a channel. `spikes_k`: spike count of a token in a channel. `log_decay`: negative.
All inputs are finite; a program needn't handle non-finite values.
Results may differ from the reference program's by a relative error of at most 0.0051.
Values may be sent and summed in bfloat16 or wider, within the bound.
No kernel may reach another device: no remote copies, remote signals or barrier semaphores. Data moves between devices by JAX's collectives and lax.ppermute only.
A program may use at most 128 MiB of HBM per device.

```python
import math
import jax
import jax.numpy as jnp
from jax import lax

D = 3584
ATTENTION_COUNT = 28
HEAD_DIM = 128
TOK_DEV = 512
FEAT = 3584
BLOCK = 512
STRING_LENGTH = 4096
STRING_COUNT = 2


def draw_log_decay(key, part):
    string_currents = jax.random.split(key, 7)
    fast_share = 0.45
    fast_heads = jax.random.uniform(string_currents[0], (STRING_COUNT, ATTENTION_COUNT, 1), jnp.float32) < fast_share
    slow_rate = math.log(2.0) / STRING_LENGTH * jnp.exp(jax.random.uniform(string_currents[1], (STRING_COUNT, ATTENTION_COUNT, 1), jnp.float32, math.log(0.3), 0.0))
    fast_rate = 1.0 / (TOK_DEV * jax.random.uniform(string_currents[2], (STRING_COUNT, ATTENTION_COUNT, 1), jnp.float32, 0.06, 0.1))
    resting_frequency = jnp.where(fast_heads, fast_rate, slow_rate)
    position = jnp.arange(STRING_LENGTH).astype(jnp.float32)
    slope_scaling_factor = 0.5 + position / STRING_LENGTH
    roughness_measure = jnp.exp(jax.random.uniform(string_currents[3], (STRING_COUNT, ATTENTION_COUNT, STRING_LENGTH), jnp.float32, math.log(0.5), math.log(2.0)))
    leading_index = jax.random.randint(string_currents[4], (STRING_COUNT, 1, 1), 0, STRING_LENGTH)
    place_offset = jax.random.randint(string_currents[6], (STRING_COUNT, 1, 1), 1, STRING_LENGTH)
    trailing_index = (leading_index + place_offset) % STRING_LENGTH
    cluster_indices = jnp.concatenate([leading_index, trailing_index], axis=-1)
    spike_cluster_list = jnp.sum((jnp.arange(STRING_LENGTH)[None, None, :, None] == cluster_indices[:, :, None, :]).astype(jnp.float32), axis=-1)
    cluster_cost_factor = jax.random.uniform(string_currents[5], (STRING_COUNT, ATTENTION_COUNT, 1), jnp.float32, 0.2, 0.5)
    return -(resting_frequency * slope_scaling_factor[None, None, :] * roughness_measure) + spike_cluster_list * jnp.log(1.0 - cluster_cost_factor)


def set_ends(result, own_key, low, high):
    longest = result.shape.index(max(result.shape))
    spots = []
    for shift in (0, 1):
        where = [jax.random.randint(jax.random.fold_in(own_key, axis), (), 0, length) for axis, length in enumerate(result.shape)]
        where[longest] = (where[longest] + shift) % result.shape[longest]
        spots.append(tuple(where))
    return result.at[spots[0]].set(low).at[spots[1]].set(high)


def raised(values, key, source, target, shards_of, factor):
    def block_of(axis_at):
        return (jnp.arange(values.shape[axis_at]) // (values.shape[axis_at] // shards_of)).reshape((-1,) + (1,) * (values.ndim - 1 - axis_at))

    first = jax.random.permutation(key, shards_of)[block_of(target)]
    second = (block_of(target) + shards_of // 2) % shards_of
    return jnp.where((block_of(source) == first) | (block_of(source) == second), factor * values, values)


def block_scale(rng, shape, pieces, low, high):
    level, own = 1.0, jax.random.fold_in(rng, 6)
    for dim, blocks in pieces:
        draws = jnp.exp(jax.random.uniform(jax.random.fold_in(own, dim), (blocks,), jnp.float32, low / len(pieces), high / len(pieces)))
        level = level * jnp.repeat(draws, shape[dim] // blocks).reshape([-1 if axis == dim else 1 for axis in range(len(shape))])
    return level


def gaussian(key, extent, width, reach, cuts=(), dtype=jnp.bfloat16):
    drawn = width * jax.random.normal(key, extent, jnp.float32)
    if cuts:
        drawn = drawn * block_scale(key, extent, cuts, -0.22, 0.18)
    return jnp.clip(drawn, -reach, reach).astype(dtype)


def heavy_noise(rng, extent, scale, most, cuts, heavy, kind=jnp.bfloat16):
    drawn = scale * jax.random.normal(rng, extent, jnp.float32)
    if cuts:
        drawn = drawn * block_scale(rng, extent, cuts, -0.22, 0.18)
    return jnp.clip(raised(drawn, jax.random.fold_in(rng, 3), *heavy), -most, most).astype(kind)


def setup_inputs(seed: int = 0) -> dict:
    key_list = jax.random.split(jax.random.key(seed), 7)
    inputs = heavy_noise(key_list[0], (STRING_COUNT, STRING_LENGTH, D), 1.0, 6.0, ((0, 2), (1, 8), (2, 2)), (1, 2, 8, 2.0))
    value_weight = gaussian(key_list[1], (D, FEAT), D ** -0.5, 0.09375, ((1, 2),))
    cotangent = gaussian(key_list[2], (STRING_COUNT, STRING_LENGTH, FEAT), 1.0, 6.0, ((0, 2), (1, 8), (2, 2)))
    spikes_q = set_ends(jax.random.randint(key_list[3], (STRING_COUNT, STRING_LENGTH, FEAT), 0, 4), jax.random.fold_in(key_list[3], 1), 0, 3).astype(jnp.int32)
    spikes_k = set_ends(jax.random.randint(key_list[4], (STRING_COUNT, STRING_LENGTH, FEAT), 0, 4), jax.random.fold_in(key_list[4], 1), 0, 3).astype(jnp.int32)
    log_decay = draw_log_decay(jax.random.fold_in(key_list[6], 71), 0)
    return {"inputs": inputs, "value_weight": value_weight, "cotangent": cotangent, "spikes_q": spikes_q, "spikes_k": spikes_k, "log_decay": log_decay}


def head_grads(query_spikes, key_spikes, out_grads, log_rates):
    queries = query_spikes.astype(jnp.float32)
    keys_f = key_spikes.astype(jnp.float32)
    grads_f = out_grads.astype(jnp.float32)
    cumulative = jnp.cumsum(log_rates, axis=1)
    scores = jnp.einsum('ntd,nsd->nts', queries, keys_f, precision=lax.Precision.HIGHEST)
    causal = jnp.arange(BLOCK)[:, None] >= jnp.arange(BLOCK)[None, :]
    log_gaps = jnp.where(causal[None], cumulative[:, :, None] - cumulative[:, None, :], -jnp.inf)
    weighted = (scores * jnp.exp(log_gaps)).astype(jnp.bfloat16)
    local_part = jnp.einsum('nts,nte->nse', weighted.astype(jnp.float32), grads_f, precision=lax.Precision.HIGHEST)
    state_terms = jnp.einsum('ntd,nte->nde', queries * jnp.exp(cumulative)[:, :, None], grads_f, precision=lax.Precision.HIGHEST)
    block_decay = jnp.exp(cumulative[:, -1])

    def backward_step(carry_state, item):
        decay_now, term_now = item
        return (term_now + decay_now * carry_state, carry_state)
    _, carry_in = lax.scan(backward_step, jnp.zeros((HEAD_DIM, HEAD_DIM), jnp.float32), (block_decay, state_terms), reverse=True)
    carried = jnp.exp(cumulative[:, -1:] - cumulative)[:, :, None] * jnp.einsum('nsd,nde->nse', keys_f, carry_in, precision=lax.Precision.HIGHEST)
    return local_part + carried

def reference(inputs, value_weight, cotangent, spikes_q, spikes_k, log_decay):
    block_count = STRING_LENGTH // BLOCK
    grad_scale = 1.0 / (2.25 * HEAD_DIM * math.sqrt(STRING_LENGTH))
    weight_total = jnp.zeros((D, FEAT), jnp.float32)
    input_rows = []
    for sequence in range(STRING_COUNT):
        query_all = spikes_q[sequence].reshape(block_count, BLOCK, ATTENTION_COUNT, HEAD_DIM)
        key_all = spikes_k[sequence].reshape(block_count, BLOCK, ATTENTION_COUNT, HEAD_DIM)
        grad_all = cotangent[sequence].reshape(block_count, BLOCK, ATTENTION_COUNT, HEAD_DIM)
        rates_all = log_decay[sequence].reshape(ATTENTION_COUNT, block_count, BLOCK)

        def one_head(head_index):
            return head_grads(lax.dynamic_index_in_dim(query_all, head_index, 2, False), lax.dynamic_index_in_dim(key_all, head_index, 2, False), lax.dynamic_index_in_dim(grad_all, head_index, 2, False), lax.dynamic_index_in_dim(rates_all, head_index, 0, False))
        per_head = lax.map(one_head, jnp.arange(ATTENTION_COUNT).astype(jnp.int32))
        value_grad = (grad_scale * per_head).astype(jnp.bfloat16)
        value_grad = value_grad.transpose(1, 2, 0, 3).reshape(STRING_LENGTH, FEAT)
        input_rows.append(jnp.dot(value_grad, value_weight.T, preferred_element_type=jnp.float32).astype(jnp.bfloat16))
        weight_total = weight_total + jnp.dot(inputs[sequence].T, value_grad, preferred_element_type=jnp.float32)
    grad_input = jnp.stack(input_rows, axis=0)
    grad_weight = weight_total * (1.0 / math.sqrt(STRING_COUNT * STRING_LENGTH))
    return (grad_input, grad_weight)
```

```python
import functools
import math

import jax
import jax.numpy as jnp
from jax import lax
from jax.experimental import pallas as pl
from jax.experimental.pallas import tpu as pltpu
from jax.sharding import PartitionSpec as P

BF = jnp.bfloat16
F32 = jnp.float32
HD = 128
PLANE = 16
EXTRA = 3 * PLANE
PARAMS = pltpu.CompilerParams(vmem_limit_bytes=56 * 1024 * 1024)
VM = pl.BlockSpec(memory_space=pltpu.VMEM)
SM = pl.BlockSpec(memory_space=pltpu.SMEM)


def dot(a, b, contract):
    return lax.dot_general(a, b, (contract, ((), ())), preferred_element_type=F32)


def hi_lo(x):
    hi = x.astype(BF)
    return hi, (x - hi.astype(F32)).astype(BF)


def transpose_kernel(a_ref, o_ref):
    o_ref[...] = a_ref[...].T


def transposed(a):
    rows, cols = a.shape
    tile = 256 if cols % 256 == 0 else 128
    return pl.pallas_call(
        transpose_kernel,
        grid=(cols // tile,),
        in_specs=[pl.BlockSpec((rows, tile), lambda i: (0, i))],
        out_specs=pl.BlockSpec((tile, rows), lambda i: (i, 0)),
        out_shape=jax.ShapeDtypeStruct((cols, rows), a.dtype),
        compiler_params=PARAMS,
        name="transpose_inputs",
    )(a)


def state_kernel(first, heads, q_ref, c_ref, ld_ref, pay_ref, own_ref, cum_ref, cumt_ref):
    tokens = ld_ref.shape[1]
    x = ld_ref[first : first + heads, :]
    x = jnp.concatenate([x, jnp.zeros((PLANE - heads, tokens), F32)], axis=0)
    lane = lax.broadcasted_iota(jnp.int32, x.shape, 1)
    shift = 1
    while shift < tokens:
        x = x + jnp.where(lane >= shift, pltpu.roll(x, shift, 1), 0.0)
        shift *= 2
    cum_ref[...] = x
    xt = jnp.concatenate([x, jnp.zeros((HD - PLANE, tokens), F32)], axis=0).T
    cumt_ref[...] = xt
    et = jnp.exp(xt)
    d = jnp.broadcast_to(jnp.exp(x[:, tokens - 1 : tokens]), (PLANE, HD))
    d_hi, d_mid = hi_lo(d)
    d_lo = (d - d_hi.astype(F32) - d_mid.astype(F32)).astype(BF)
    at = heads * HD
    pay_ref[at : at + PLANE, :] = d_hi
    pay_ref[at + PLANE : at + 2 * PLANE, :] = d_mid
    pay_ref[at + 2 * PLANE : at + EXTRA, :] = d_lo
    own_ref[at : at + PLANE, :] = d
    own_ref[at + PLANE : at + EXTRA, :] = jnp.zeros((EXTRA - PLANE, HD), F32)
    for h in range(heads):
        s = slice(h * HD, (h + 1) * HD)
        q = q_ref[:, s].astype(F32).astype(BF)
        hi, lo = hi_lo(c_ref[:, s].astype(F32) * et[:, h : h + 1])
        both = dot(q, jnp.concatenate([hi, lo], axis=1), ((0,), (0,)))
        term = both[:, :HD] + both[:, HD:]
        own_ref[s, :] = term
        pay_ref[s, :] = term.astype(BF)


def state_terms(group, heads, q, c, ld):
    tokens = q.shape[0]
    rows = heads * HD + EXTRA
    cols = pl.BlockSpec((tokens, heads * HD), lambda i: (0, group))
    whole = lambda shape: pl.BlockSpec(shape, lambda i: (0, 0))
    return pl.pallas_call(
        functools.partial(state_kernel, group * heads, heads),
        grid=(1,),
        in_specs=[cols, cols, whole(ld.shape)],
        out_specs=[whole((rows, HD)), whole((rows, HD)), whole((PLANE, tokens)), whole((tokens, HD))],
        out_shape=[
            jax.ShapeDtypeStruct((rows, HD), BF),
            jax.ShapeDtypeStruct((rows, HD), F32),
            jax.ShapeDtypeStruct((PLANE, tokens), F32),
            jax.ShapeDtypeStruct((tokens, HD), F32),
        ],
        compiler_params=PARAMS,
        name="state_terms",
    )(q, c, ld)


def decays(ref, heads):
    p = ref[heads * HD :, :].astype(F32)
    return p[:PLANE] + p[PLANE : 2 * PLANE] + p[2 * PLANE :]


def append_kernel(heads, swap_ref, a_ref, b_ref, pay_ref, own_ref):
    swap = swap_ref[0] != 0
    da, db = decays(a_ref, heads), decays(b_ref, heads)
    one = jnp.ones_like(da)
    scale_a = jnp.where(swap, db, one)
    scale_b = jnp.where(swap, one, da)
    d = da * db
    d_hi, d_mid = hi_lo(d)
    d_lo = (d - d_hi.astype(F32) - d_mid.astype(F32)).astype(BF)
    at = heads * HD
    pay_ref[at : at + PLANE, :] = d_hi
    pay_ref[at + PLANE : at + 2 * PLANE, :] = d_mid
    pay_ref[at + 2 * PLANE : at + EXTRA, :] = d_lo
    own_ref[at : at + PLANE, :] = d
    own_ref[at + PLANE : at + EXTRA, :] = jnp.zeros((EXTRA - PLANE, HD), F32)
    for h in range(heads):
        s = slice(h * HD, (h + 1) * HD)
        term = scale_a[h : h + 1] * a_ref[s, :].astype(F32) + scale_b[h : h + 1] * b_ref[s, :].astype(F32)
        own_ref[s, :] = term
        pay_ref[s, :] = term.astype(BF)


def append(heads, swap, a, b):
    return pl.pallas_call(
        functools.partial(append_kernel, heads),
        in_specs=[SM, VM, VM],
        out_specs=[VM, VM],
        out_shape=[jax.ShapeDtypeStruct(a.shape, BF), jax.ShapeDtypeStruct(a.shape, F32)],
        compiler_params=PARAMS,
        name="join_states",
    )(swap, a, b)


def local_kernel(heads, q_ref, k_ref, c_ref, cum_ref, cumt_ref, o_ref):
    tokens = q_ref.shape[0]
    tile = 128
    for h in range(heads):
        s = slice(h * HD, (h + 1) * HD)
        q = q_ref[:, s].astype(F32).astype(BF)
        k = k_ref[:, s].astype(F32).astype(BF)
        c = c_ref[:, s]
        for at in range(0, tokens, tile):
            scores = dot(k[at : at + tile], q[at:], ((1,), (1,)))
            gap = cum_ref[h : h + 1, at:] - cumt_ref[at : at + tile, h : h + 1]
            row = lax.broadcasted_iota(jnp.int32, gap.shape, 0)
            col = lax.broadcasted_iota(jnp.int32, gap.shape, 1)
            gap = jnp.where(col >= row, gap, -jnp.inf)
            weighted = (scores * jnp.exp(gap)).astype(BF)
            o_ref[at : at + tile, s] = dot(weighted, c[at:], ((1,), (0,)))


def local_part(group, heads, q, k, c, cum, cumt):
    tokens = q.shape[0]
    cols = pl.BlockSpec((tokens, heads * HD), lambda i: (0, group))
    whole = lambda shape: pl.BlockSpec(shape, lambda i: (0, 0))
    return pl.pallas_call(
        functools.partial(local_kernel, heads),
        grid=(1,),
        in_specs=[cols, cols, cols, whole(cum.shape), whole(cumt.shape)],
        out_specs=whole((tokens, heads * HD)),
        out_shape=jax.ShapeDtypeStruct((tokens, heads * HD), F32),
        compiler_params=PARAMS,
        name="local_part",
    )(q, k, c, cum, cumt)


def value_kernel(heads, chunks, scale, first_ref, k_ref, l_ref, cumt_ref, oth_ref, e_ref, r_ref, *outs):
    tokens = k_ref.shape[0]
    first = first_ref[0] != 0
    de = decays(e_ref, heads)
    do = decays(oth_ref, heads)
    use_oth = jnp.where(first, 1.0, 0.0)
    scale_e = jnp.where(first, do, jnp.ones_like(do))
    fall = jnp.exp(cumt_ref[tokens - 1 : tokens, :] - cumt_ref[...])
    h = 0
    for out, count in zip(outs, chunks):
        for j in range(count):
            s = slice(h * HD, (h + 1) * HD)
            e = e_ref[s, :].astype(F32) + de[h : h + 1] * r_ref[s, :].astype(F32)
            carry = use_oth * oth_ref[s, :].astype(F32) + scale_e[h : h + 1] * e
            hi, lo = hi_lo(carry)
            k = k_ref[:, s].astype(F32).astype(BF)
            both = dot(k, jnp.concatenate([hi, lo], axis=1), ((1,), (0,)))
            carried = fall[:, h : h + 1] * (both[:, :HD] + both[:, HD:])
            out[:, j * HD : (j + 1) * HD] = (scale * (l_ref[:, s] + carried)).astype(BF)
            h += 1


def value_grads(group, heads, chunks, scale, first, k, local, cumt, oth, e, r):
    tokens = k.shape[0]
    cols = pl.BlockSpec((tokens, heads * HD), lambda i: (0, group))
    whole = lambda shape: pl.BlockSpec(shape, lambda i: (0, 0))
    return pl.pallas_call(
        functools.partial(value_kernel, heads, chunks, scale),
        grid=(1,),
        in_specs=[SM, cols] + [whole(a.shape) for a in (local, cumt, oth, e, r)],
        out_specs=[whole((tokens, n * HD)) for n in chunks],
        out_shape=[jax.ShapeDtypeStruct((tokens, n * HD), BF) for n in chunks],
        compiler_params=PARAMS,
        name="value_grad",
    )(first, k, local, cumt, oth, e, r)


def input_kernel(at_ref, *refs):
    vs, w_ref, o_ref = refs[:-2], refs[-2], refs[-1]
    start, total = 0, None
    for v in vs:
        width = v.shape[1]
        part = dot(v[...], w_ref[:, start : start + width], ((1,), (1,)))
        total = part if total is None else total + part
        start += width
    o_ref[...] = total.astype(o_ref.dtype)


def input_part(at, vs, w, rows_here, dtype):
    tokens = vs[0].shape[0]
    tile = 256 if rows_here % 256 == 0 else 128
    tiles = rows_here // tile
    spec = pltpu.PrefetchScalarGridSpec(
        num_scalar_prefetch=1,
        grid=(tiles,),
        in_specs=[pl.BlockSpec(v.shape, lambda n, at: (0, 0)) for v in vs]
        + [pl.BlockSpec((tile, w.shape[1]), lambda n, at: (at[0] * tiles + n, 0))],
        out_specs=pl.BlockSpec((tokens, tile), lambda n, at: (0, n)),
    )
    return pl.pallas_call(
        input_kernel,
        grid_spec=spec,
        out_shape=jax.ShapeDtypeStruct((tokens, rows_here), dtype),
        compiler_params=PARAMS,
        name="input_part",
    )(at, *vs, w)


def weight_kernel(side_ref, low_ref, a_ref, v00, v01, v10, v11, o_ref):
    total = None
    for i, vs in enumerate(((v00, v01), (v10, v11))):
        for j, v in enumerate(vs):
            part = dot(a_ref[0, i, j, 0], v[...], ((1,), (0,)))
            total = part if total is None else total + part
    o_ref[0] = total.astype(o_ref.dtype)


def weight_part(side, low, a, vs, dtype):
    blocks, width = side.shape[0], vs[0].shape[1]
    rows, tokens = a.shape[4:]
    spec = pltpu.PrefetchScalarGridSpec(
        num_scalar_prefetch=2,
        grid=(blocks,),
        in_specs=[pl.BlockSpec((1, 2, 2, 1, rows, tokens), lambda n, side, low: (side[n], 0, 0, low[n], 0, 0))]
        + [pl.BlockSpec(v.shape, lambda n, side, low: (0, 0)) for v in vs],
        out_specs=pl.BlockSpec((1, rows, width), lambda n, side, low: (n, 0, 0)),
    )
    return pl.pallas_call(
        weight_kernel,
        grid_spec=spec,
        out_shape=jax.ShapeDtypeStruct((blocks, rows, width), dtype),
        compiler_params=PARAMS,
        name="weight_part",
    )(side, low, a, *vs)


def swap_with(x, axis, bit):
    return lax.ppermute(x, axis, [(i, i ^ bit) for i in range(lax.axis_size(axis))])


def from_later(x, axis, shift):
    return lax.ppermute(x, axis, [(i, i - shift) for i in range(shift, lax.axis_size(axis))])


def pick(x, at, axis):
    return lax.dynamic_index_in_dim(x, at, axis, keepdims=False)


def local(inputs, value_weight, cotangent, spikes_q, spikes_k, log_decay):
    seqs, sides, dps = lax.axis_size("seq"), lax.axis_size("head"), lax.axis_size("dp")
    seq, side, dp = lax.axis_index("seq"), lax.axis_index("head"), lax.axis_index("dp")
    y, z = seq % 2, seq // 2
    tokens, rows_here = inputs.shape[1:]
    features = value_weight.shape[1]
    heads_here = log_decay.shape[1]
    seq_length = tokens * seqs
    grad_scale = 1.0 / (2.25 * HD * math.sqrt(seq_length))
    groups = 2 if heads_here % 2 == 0 else 1
    heads = heads_here // groups
    chunks = (heads - heads // 2, heads // 2)
    rows = rows_here * sides // (seqs * dps)
    lows = rows_here // (2 * dps * rows)
    stages = (seqs // 2).bit_length() - 1
    y_flag = y.astype(jnp.int32).reshape(1)
    zero_flag = jnp.zeros((1,), jnp.int32)
    first_flag = 1 - y_flag

    q, k, c, ld = spikes_q[0], spikes_k[0], cotangent[0], log_decay[0]

    own = [state_terms(g, heads, q, c, ld) for g in range(groups)]
    other = [swap_with(own[g][0], "seq", 1) for g in range(groups)]

    a = transposed(inputs[0]).reshape(lows, 2, dps, rows, tokens)
    a = jnp.stack([pick(a, y, 1), swap_with(pick(a, 1 - y, 1), "seq", 1)])
    a = jnp.stack([pick(a, dp, 2), swap_with(pick(a, 1 - dp, 2), "dp", 1)])
    a = jnp.stack([a] + [swap_with(a, "head", i) for i in range(1, sides)])

    joined = [append(heads, y_flag, own[g][1], other[g]) for g in range(groups)]
    locals_ = [local_part(g, heads, q, k, c, own[g][2], own[g][3]) for g in range(groups)]
    values = []
    for g in range(groups):
        pay, mine = joined[g]
        e = None
        for stage in range(stages):
            later = from_later(pay, "seq", 2 << stage)
            if stage == 0:
                e = later
            elif stage < stages - 1:
                e = append(heads, zero_flag, e, later)[1]
            if stage < stages - 1:
                pay, mine = append(heads, zero_flag, mine, later)
        last = later if stages > 1 else jnp.zeros_like(later)
        values.append(
            value_grads(g, heads, chunks, grad_scale, first_flag, k, locals_[g], own[g][3], other[g], e, last)
        )
    values = [v for vs in values for v in vs]

    order = [0]
    for stage in range(stages):
        order = [o for o in order] + [o | (1 << stage) for o in order]
    order = [int(format(o, "b").zfill(stages)[::-1], 2) for o in order]
    at_z = jnp.stack([z ^ o for o in order]).astype(jnp.int32)
    block_side = (at_z // lows) ^ side
    block_low = at_z % lows
    half = len(order) // 2

    results = []
    for v in values:
        from_y = swap_with(v, "seq", 1)
        parts = (v, from_y, swap_with(v, "dp", 1), swap_with(from_y, "dp", 1))
        away = weight_part(block_side[half:], block_low[half:], a, parts, BF)
        came = swap_with(away, "seq", 2)
        keep = weight_part(block_side[:half], block_low[:half], a, parts, F32)
        for stage in range(1, stages):
            n = keep.shape[0] // 2
            away = (keep[n:] + came[n:].astype(F32)).astype(BF)
            keep = keep[:n] + came[:n].astype(F32)
            came = swap_with(away, "seq", 2 << stage)
        results.append(keep[0] + came[0].astype(F32))
    grad_weight = jnp.concatenate(results, axis=1) * (1.0 / math.sqrt(dps * seq_length))

    total = None
    at = [(side ^ i).astype(jnp.int32).reshape(1) for i in range(sides)]
    sent = [swap_with(input_part(at[i], values, value_weight, rows_here, BF), "head", i) for i in range(1, sides)]
    total = input_part(at[0], values, value_weight, rows_here, F32)
    for s in sent:
        total = total + s.astype(F32)
    return total.astype(BF)[None], grad_weight


def solution(mesh):
    return jax.shard_map(
        local,
        mesh=mesh,
        in_specs=(
            P("dp", "seq", "head"),
            P(None, "head"),
            P("dp", "seq", "head"),
            P("dp", "seq", "head"),
            P("dp", "seq", "head"),
            P("dp", "head", "seq"),
        ),
        out_specs=(P("dp", "seq", "head"), P(("seq", "dp"), "head")),
        check_vma=False,
    )
```

```python
import functools
import math

import jax
import jax.numpy as jnp
from jax import lax
from jax.experimental import pallas as pl
from jax.experimental.pallas import tpu as pltpu
from jax.sharding import PartitionSpec as P

BF = jnp.bfloat16
F32 = jnp.float32
HD = 128
PLANE = 16
EXTRA = 3 * PLANE
PARAMS = pltpu.CompilerParams(vmem_limit_bytes=20 * 1024 * 1024)
VM = pl.BlockSpec(memory_space=pltpu.VMEM)
SM = pl.BlockSpec(memory_space=pltpu.SMEM)
ANY = pl.BlockSpec(memory_space=pl.ANY)


def dot(a, b, contract):
    return lax.dot_general(a, b, (contract, ((), ())), preferred_element_type=F32)


def hi_lo(x):
    hi = x.astype(BF)
    return hi, (x - hi.astype(F32)).astype(BF)


def cost(microseconds):
    return pl.CostEstimate(flops=int(microseconds * 1.15e9), transcendentals=0, bytes_accessed=0)


def call(kernel, name, us, outs, smalls, arrays, after=(), scratch=(), far=()):
    def body(*refs):
        refs = list(refs)
        first = len(smalls) + len(arrays) + len(far)
        kernel(*refs[:first], *refs[first + len(after) :])

    return pl.pallas_call(
        body,
        in_specs=[SM] * len(smalls) + [VM] * len(arrays) + [ANY] * (len(far) + len(after)),
        out_specs=[VM] * len(outs),
        out_shape=[jax.ShapeDtypeStruct(shape, dtype) for shape, dtype in outs],
        scratch_shapes=list(scratch),
        compiler_params=PARAMS,
        cost_estimate=cost(us),
        name=name,
    )(*smalls, *arrays, *far, *after)


def transpose_kernel(lows, rows, at_ref, a_ref, near_ref, far_ref, flat):
    flat[...] = a_ref[...].T.astype(flat.dtype)
    for yr, out in enumerate((near_ref, far_ref)):
        for dr in range(2):
            for low in range(lows):
                start = ((low * 2 + (at_ref[0] ^ yr)) * 2 + (at_ref[1] ^ dr)) * rows
                out[low, dr] = flat[pl.ds(pl.multiple_of(start, 8), rows), :].astype(BF)


def transposed(at, a, lows, rows, after):
    tokens, cols = a.shape
    outs = [((lows, 2, rows, tokens), BF)] * 2
    scratch = [pltpu.VMEM((cols, tokens), BF if rows % 16 == 0 else F32)]
    return call(functools.partial(transpose_kernel, lows, rows), "transpose_inputs", 1.2, outs, [at], [a], after, scratch)


def state_kernel(group, heads, cols, q_ref, c_ref, ld_ref, pay_ref, own_ref, cum_ref, cumt_ref):
    tokens = ld_ref.shape[1]
    x = ld_ref[group * heads : (group + 1) * heads, :]
    x = jnp.concatenate([x, jnp.zeros((PLANE - heads, tokens), F32)], axis=0)
    lane = lax.broadcasted_iota(jnp.int32, x.shape, 1)
    shift = 1
    while shift < tokens:
        x = x + jnp.where(lane >= shift, pltpu.roll(x, shift, 1), 0.0)
        shift *= 2
    cum_ref[...] = x
    xt = jnp.concatenate([x, jnp.zeros((HD - PLANE, tokens), F32)], axis=0).T
    cumt_ref[...] = xt
    et = jnp.exp(xt)
    d = jnp.broadcast_to(jnp.exp(x[:, tokens - 1 : tokens]), (PLANE, HD))
    put_decays(d, heads, pay_ref, own_ref)
    for h in range(heads):
        s = slice(h * HD, (h + 1) * HD)
        f = slice(cols + h * HD, cols + (h + 1) * HD)
        q = q_ref[:, f].astype(F32).astype(BF)
        hi, lo = hi_lo(c_ref[:, f].astype(F32) * et[:, h : h + 1])
        both = dot(q, jnp.concatenate([hi, lo], axis=1), ((0,), (0,)))
        term = both[:, :HD] + both[:, HD:]
        own_ref[s, :] = term
        pay_ref[s, :] = term.astype(BF)


def state_outs(heads, tokens):
    rows = heads * HD + EXTRA
    return [((rows, HD), BF), ((rows, HD), F32), ((PLANE, tokens), F32), ((tokens, HD), F32)]


def first_state_terms(heads, q, c, ld, after):
    tokens = q.shape[0]
    cols = pl.BlockSpec((tokens, heads * HD), lambda i: (0, 0))
    whole = lambda shape: pl.BlockSpec(shape, lambda i: (0, 0))
    outs = state_outs(heads, tokens)
    return pl.pallas_call(
        lambda q, c, ld, after, *outs: state_kernel(0, heads, 0, q, c, ld, *outs),
        grid=(1,),
        in_specs=[cols, cols, whole(ld.shape), ANY],
        out_specs=[whole(shape) for shape, _ in outs],
        out_shape=[jax.ShapeDtypeStruct(shape, dtype) for shape, dtype in outs],
        compiler_params=PARAMS,
        cost_estimate=cost(2.0),
        name="state_terms",
    )(q, c, ld, after)


def later_state_terms(group, heads, q, c, ld, after):
    kernel = functools.partial(state_kernel, group, heads, group * heads * HD)
    return call(kernel, "state_terms", 1.6, state_outs(heads, q.shape[0]), [], [q, c, ld], after)


def put_decays(d, heads, pay_ref, own_ref):
    d_hi, d_mid = hi_lo(d)
    d_lo = (d - d_hi.astype(F32) - d_mid.astype(F32)).astype(BF)
    at = heads * HD
    pay_ref[at : at + PLANE, :] = d_hi
    pay_ref[at + PLANE : at + 2 * PLANE, :] = d_mid
    pay_ref[at + 2 * PLANE : at + EXTRA, :] = d_lo
    own_ref[at : at + PLANE, :] = d
    own_ref[at + PLANE : at + EXTRA, :] = jnp.zeros((EXTRA - PLANE, HD), F32)


def decays(ref, heads):
    p = ref[heads * HD :, :].astype(F32)
    return p[:PLANE] + p[PLANE : 2 * PLANE] + p[2 * PLANE :]


def append_kernel(heads, swap_ref, a_ref, b_ref, pay_ref, own_ref):
    swap = swap_ref[0] != 0
    da, db = decays(a_ref, heads), decays(b_ref, heads)
    one = jnp.ones_like(da)
    scale_a = jnp.where(swap, db, one)
    scale_b = jnp.where(swap, one, da)
    put_decays(da * db, heads, pay_ref, own_ref)
    for h in range(heads):
        s = slice(h * HD, (h + 1) * HD)
        term = scale_a[h : h + 1] * a_ref[s, :].astype(F32) + scale_b[h : h + 1] * b_ref[s, :].astype(F32)
        own_ref[s, :] = term
        pay_ref[s, :] = term.astype(BF)


def append(heads, swap, a, b, after=()):
    outs = [(a.shape, BF), (a.shape, F32)]
    return call(functools.partial(append_kernel, heads), "join_states", 0.9, outs, [swap], [a, b], after)


def local_kernel(heads, cols, q_ref, k_ref, c_ref, cum_ref, cumt_ref, o_ref):
    tokens = q_ref.shape[0]
    tile = 256
    row = lax.broadcasted_iota(jnp.int32, (tile, tile), 0)
    col = lax.broadcasted_iota(jnp.int32, (tile, tile), 1)
    causal = col >= row
    for h in range(heads):
        f = slice(cols + h * HD, cols + (h + 1) * HD)
        q = q_ref[:, f].astype(F32).astype(BF)
        k = k_ref[:, f].astype(F32).astype(BF)
        scores = dot(k, q, ((1,), (1,)))
        strips = []
        for at in range(0, tokens, tile):
            end = at + tile
            before = cumt_ref[at:end, h : h + 1]
            gap = jnp.where(causal, cum_ref[h : h + 1, at:end] - before, -jnp.inf)
            strip = [jnp.zeros((tile, at), BF)] if at else []
            strip.append((scores[at:end, at:end] * jnp.exp(gap)).astype(BF))
            if end < tokens:
                middle = cum_ref[h : h + 1, end - 1 : end]
                to_t = jnp.exp(cum_ref[h : h + 1, end:] - middle)
                from_s = jnp.exp(middle - before)
                strip.append((scores[at:end, end:] * to_t * from_s).astype(BF))
            strips.append(jnp.concatenate(strip, axis=1))
        weighted = jnp.concatenate(strips, axis=0)
        o_ref[:, h * HD : (h + 1) * HD] = dot(weighted, c_ref[:, f], ((1,), (0,)))


def local_part(group, heads, q, k, c, cum, cumt, after):
    kernel = functools.partial(local_kernel, heads, group * heads * HD)
    return call(kernel, "local_part", 2.2, [((q.shape[0], heads * HD), F32)], [], [q, k, c, cum, cumt], after)[0]


def value_kernel(heads, cols, scale, first_ref, k_ref, l_ref, cumt_ref, oth_ref, e_ref, r_ref, o_ref):
    tokens = k_ref.shape[0]
    first = first_ref[0] != 0
    de = decays(e_ref, heads)
    do = decays(oth_ref, heads)
    use_oth = jnp.where(first, 1.0, 0.0)
    scale_e = jnp.where(first, do, jnp.ones_like(do))
    fall = jnp.exp(cumt_ref[tokens - 1 : tokens, :] - cumt_ref[...])
    for h in range(heads):
        s = slice(h * HD, (h + 1) * HD)
        e = e_ref[s, :].astype(F32) + de[h : h + 1] * r_ref[s, :].astype(F32)
        carry = use_oth * oth_ref[s, :].astype(F32) + scale_e[h : h + 1] * e
        hi, lo = hi_lo(carry)
        k = k_ref[:, cols + h * HD : cols + (h + 1) * HD].astype(F32).astype(BF)
        both = dot(k, jnp.concatenate([hi, lo], axis=1), ((1,), (0,)))
        carried = fall[:, h : h + 1] * (both[:, :HD] + both[:, HD:])
        o_ref[:, s] = (scale * (l_ref[:, s] + carried)).astype(BF)


def value_grads(group, heads, scale, first, k, local, cumt, oth, e, r, after):
    kernel = functools.partial(value_kernel, heads, group * heads * HD, scale)
    outs = [((k.shape[0], heads * HD), BF)]
    return call(kernel, "value_grad", 0.8, outs, [first], [k, local, cumt, oth, e, r], after)[0]


def input_kernel(rows, sides, side_ref, *refs):
    vs, w_ref, outs, v_all, w_all, sems = refs[: -(4 + sides)], refs[-(4 + sides)], refs[-(3 + sides) : -3], *refs[-3:]
    half = rows // 2
    copies = []
    for i in range(2 * sides):
        start = ((side_ref[0] ^ ((i // 2 + 1) % sides)) * 2 + i % 2) * half
        start = pl.multiple_of(start, 64)
        copies.append(pltpu.make_async_copy(w_ref.at[pl.ds(start, half)], w_all.at[i], sems.at[i]))
        copies[-1].start()
    start = 0
    for v in vs:
        v_all[:, start : start + v.shape[1]] = v[...]
        start += v.shape[1]
    for i, copy in enumerate(copies):
        copy.wait()
        out = outs[i // 2]
        part = dot(v_all[...], w_all[i], ((1,), (1,)))
        out[:, i % 2 * half : (i % 2 + 1) * half] = part.astype(out.dtype)


def input_parts(side, sides, vs, w, after):
    tokens, features, rows = vs[0].shape[0], w.shape[1], w.shape[0] // sides
    outs = [((tokens, rows), BF)] * (sides - 1) + [((tokens, rows), F32)]
    scratch = [
        pltpu.VMEM((tokens, features), BF),
        pltpu.VMEM((2 * sides, rows // 2, features), BF),
        pltpu.SemaphoreType.DMA((2 * sides,)),
    ]
    kernel = functools.partial(input_kernel, rows, sides)
    return call(kernel, "input_part", 8.0, outs, [side], vs, after, scratch, [w])


def weight_kernel(blocks, sides, start, side_ref, low_ref, *refs):
    pieces = [refs[2 * s : 2 * s + 2] for s in range(sides)]
    v_ref, v_y_ref, away_ref, keep_ref, all_v = refs[2 * sides :]
    tokens, width = v_ref.shape[0], away_ref.shape[2]
    all_v[:tokens, :] = v_ref[:, start : start + width]
    all_v[tokens:, :] = v_y_ref[:, start : start + width]
    for n in range(blocks):
        for s in range(sides):

            @pl.when(side_ref[n] == s)
            def _(n=n, s=s):
                a = [p[low_ref[n]] for p in pieces[s]]
                rows = a[0].shape[1]
                a = jnp.concatenate([jnp.concatenate([p[1], p[0]], axis=0) for p in a], axis=1)
                total = dot(a, all_v[...], ((1,), (0,)))
                away_ref[n] = total[:rows].astype(BF)
                keep_ref[n] = total[rows:]


def weight_part(side, low, pieces, vs, start, width, after):
    blocks, sides = side.shape[0], len(pieces)
    rows = pieces[0][0].shape[2]
    shape = (blocks, rows, width)
    scratch = [pltpu.VMEM((2 * vs[0].shape[0], width), BF)]
    arrays = [p for side_pieces in pieces for p in side_pieces] + list(vs)
    kernel = functools.partial(weight_kernel, blocks, sides, start)
    return call(kernel, "weight_part", 3.2, [(shape, BF), (shape, F32)], [side, low], arrays, after, scratch)


def fold_kernel(keep_ref, came_ref, away_ref, left_ref):
    half = away_ref.shape[0]
    left_ref[...] = keep_ref[:half] + came_ref[:half].astype(F32)
    away_ref[...] = (keep_ref[half:] + came_ref[half:].astype(F32)).astype(BF)


def fold(keep, came, after):
    blocks, rows, width = keep.shape
    shape = (blocks // 2, rows, width)
    return call(fold_kernel, "fold_weight", 1.0, [(shape, BF), (shape, F32)], [], [keep, came], after)


def tied(x, *after):
    return lax.optimization_barrier((x, *after))[0]


def swap_with(x, axis, bit):
    return lax.ppermute(x, axis, [(i, i ^ bit) for i in range(lax.axis_size(axis))])


def from_later(x, axis, shift):
    return lax.ppermute(x, axis, [(i, i - shift) for i in range(shift, lax.axis_size(axis))])


def local(inputs, value_weight, cotangent, spikes_q, spikes_k, log_decay):
    seqs, sides, dps = lax.axis_size("seq"), lax.axis_size("head"), lax.axis_size("dp")
    seq, side, dp = lax.axis_index("seq"), lax.axis_index("head"), lax.axis_index("dp")
    y, z = seq % 2, seq // 2
    tokens, rows_here = inputs.shape[1:]
    features = value_weight.shape[1]
    heads_here = log_decay.shape[1]
    seq_length = tokens * seqs
    grad_scale = 1.0 / (2.25 * HD * math.sqrt(seq_length))
    groups = 2 if heads_here % 2 == 0 else 1
    heads = heads_here // groups
    chunks = (heads - heads // 2, heads // 2)
    rows = rows_here * sides // (seqs * dps)
    lows = rows_here // (2 * dps * rows)
    stages = (seqs // 2).bit_length() - 1
    y_flag = y.astype(jnp.int32).reshape(1)
    zero_flag = jnp.zeros((1,), jnp.int32)
    first_flag = 1 - y_flag
    place = jnp.stack([y, dp]).astype(jnp.int32)

    q, k, c, ld = spikes_q[0], spikes_k[0], cotangent[0], log_decay[0]

    near, far = transposed(place, inputs[0], lows, rows, ())
    near_x = [swap_with(near, "head", i) for i in range(1, sides)]

    own = [first_state_terms(heads, q, c, ld, near)]
    for g in range(1, groups):
        own.append(later_state_terms(g, heads, q, c, ld, [own[-1][0]]))
    other = [swap_with(o[0], "seq", 1) for o in own]
    far = swap_with(tied(far, other[-1]), "seq", 1)
    pieces = [[near, far]] + [[n, swap_with(far, "head", i + 1)] for i, n in enumerate(near_x)]

    last = own[-1][0]
    locals_, joined = [], []
    for g in range(groups):
        joined.append(append(heads, y_flag, own[g][1], other[g], [last]))
        last = joined[g][0]
    for g in range(groups):
        locals_.append(local_part(g, heads, q, k, c, own[g][2], own[g][3], [last, *near_x]))
        last = locals_[g]
    values = []
    for g in range(groups):
        pay, ours = joined[g]
        e = None
        for stage in range(stages):
            later = from_later(pay, "seq", 2 << stage)
            if stage == 0:
                e = later
            elif stage < stages - 1:
                e = append(heads, zero_flag, e, later)[1]
            if stage < stages - 1:
                pay, ours = append(heads, zero_flag, ours, later)
        if stages == 1:
            later = jnp.zeros_like(later)
        values.append(
            value_grads(g, heads, grad_scale, first_flag, k, locals_[g], own[g][3], other[g], e, later, [far])
        )

    order = [0]
    for stage in range(stages):
        order = order + [o | (1 << stage) for o in order]
    order = [int(format(o, "b").zfill(stages)[::-1], 2) for o in order]
    at_z = jnp.stack([z ^ o for o in order]).astype(jnp.int32)
    block_side = (at_z // lows) ^ side
    block_low = at_z % lows

    from_y = [swap_with(v, "seq", 1) for v in values]
    *others, total = input_parts(side.astype(jnp.int32).reshape(1), sides, values, value_weight, [])
    sent = [swap_with(o, "head", i + 1) for i, o in enumerate(others)]

    parts = [(g, start, n) for g in range(groups) for start, n in ((0, chunks[0]), (chunks[0], chunks[1]))]
    kept, last = [None] * len(parts), total
    for i in range(len(parts) + stages - 1):
        if i < len(parts):
            g, start, n = parts[i]
            away, keep = weight_part(
                block_side, block_low, pieces, (values[g], from_y[g]), start * HD, n * HD, [last]
            )
            came = swap_with(away, "dp", 1)
            away, keep = fold(keep, came, [])
            kept[i] = (keep, swap_with(away, "seq", 2))
            last = away
        for stage in range(1, stages):
            j = i - stage
            if 0 <= j < len(parts):
                away, keep = fold(*kept[j], [last])
                kept[j] = (keep, swap_with(away, "seq", 2 << stage))
                last = away
    results = [keep[0] + came[0].astype(F32) for keep, came in kept]
    grad_weight = jnp.concatenate(results, axis=1) * (1.0 / math.sqrt(dps * seq_length))

    for s in sent:
        total = total + s.astype(F32)
    return total.astype(BF)[None], grad_weight


def solution(mesh):
    return jax.shard_map(
        local,
        mesh=mesh,
        in_specs=(
            P("dp", "seq", "head"),
            P(None, "head"),
            P("dp", "seq", "head"),
            P("dp", "seq", "head"),
            P("dp", "seq", "head"),
            P("dp", "head", "seq"),
        ),
        out_specs=(P("dp", "seq", "head"), P(("seq", "dp"), "head")),
        check_vma=False,
    )
```

```python
import functools
import math

import jax
import jax.numpy as jnp
from jax import lax
from jax.experimental import pallas as pl
from jax.experimental.pallas import tpu as pltpu
from jax.sharding import PartitionSpec as P

BF = jnp.bfloat16
F32 = jnp.float32
HD = 128
PLANE = 16
EXTRA = 3 * PLANE
PARAMS = pltpu.CompilerParams(vmem_limit_bytes=12 * 1024 * 1024)
VM = pl.BlockSpec(memory_space=pltpu.VMEM)
SM = pl.BlockSpec(memory_space=pltpu.SMEM)
ANY = pl.BlockSpec(memory_space=pl.ANY)


def dot(a, b, contract):
    return lax.dot_general(a, b, (contract, ((), ())), preferred_element_type=F32)


def hi_lo(x):
    hi = x.astype(BF)
    return hi, (x - hi.astype(F32)).astype(BF)


LONG = pl.CostEstimate(flops=2 * 10**10, transcendentals=0, bytes_accessed=0)


class Line:
    def __init__(self):
        self.last = []

    def __call__(self, kernel, name, outs, smalls, arrays, after=(), scratch=(), cost=LONG, last=0):
        waits = [*self.last, *after]
        first = len(smalls) + len(arrays)

        def body(*refs):
            kernel(*refs[:first], *refs[first + len(waits) :])

        results = pl.pallas_call(
            body,
            in_specs=[SM] * len(smalls) + [VM] * len(arrays) + [ANY] * len(waits),
            out_specs=[VM] * len(outs),
            out_shape=[jax.ShapeDtypeStruct(shape, dtype) for shape, dtype in outs],
            scratch_shapes=list(scratch),
            compiler_params=PARAMS,
            cost_estimate=cost,
            name=name,
        )(*smalls, *arrays, *waits)
        self.last = [results[last]]
        return results


def pause_kernel(o_ref):
    o_ref[...] = jnp.zeros_like(o_ref)


def pause(line, after=(), cost=LONG):
    line(pause_kernel, "pause", [((8, HD), F32)], [], [], after, (), cost)


def copy_kernel(*refs):
    outs = refs[len(refs) // 2 :]
    for ref, out in zip(refs, outs):
        out[...] = ref[...]


def merge_kernel(counts, *refs):
    first = 0
    for count, out in zip(counts, refs[sum(counts) :]):
        start = 0
        for ref in refs[first : first + count]:
            out[start : start + ref.shape[0]] = ref[...]
            start += ref.shape[0]
        first += count


def merged(line, groups):
    outs = [((sum(p.shape[0] for p in g), *g[0].shape[1:]), g[0].dtype) for g in groups]
    kernel = functools.partial(merge_kernel, [len(g) for g in groups])
    return line(kernel, "merge_inputs", outs, [], [p for g in groups for p in g])


def transpose_kernel(order, rows, at_ref, a_ref, near_ref, *refs):
    far_refs, flat = refs[:-1], refs[-1]
    flat[...] = a_ref[...].T.astype(flat.dtype)
    each = len(order) // len(far_refs)
    for yr in range(2):
        for dr in range(2):
            for i, low in enumerate(order):
                start = (((at_ref[2] ^ low) * 2 + (at_ref[0] ^ yr)) * 2 + (at_ref[1] ^ dr)) * rows
                piece = flat[pl.ds(pl.multiple_of(start, 8), rows), :].astype(BF)
                if yr == 0:
                    near_ref[i, dr] = piece
                else:
                    far_refs[i // each][i % each, dr] = piece


def transposed(line, at, a, order, rows):
    tokens, cols = a.shape
    halves = 2 if len(order) % 2 == 0 else 1
    outs = [((len(order), 2, rows, tokens), BF)] + [((len(order) // halves, 2, rows, tokens), BF)] * halves
    scratch = [pltpu.VMEM((cols, tokens), BF if rows % 16 == 0 else F32)]
    kernel = functools.partial(transpose_kernel, order, rows)
    return line(kernel, "transpose_inputs", outs, [at], [a], (), scratch)


def state_kernel(first, heads, ld_ref, q_ref, c_ref, pay_ref, own_ref, cum_ref, cumt_ref, qbf_ref):
    tokens = ld_ref.shape[1]
    x = ld_ref[first : first + heads, :]
    x = jnp.concatenate([x, jnp.zeros((PLANE - heads, tokens), F32)], axis=0)
    lane = lax.broadcasted_iota(jnp.int32, x.shape, 1)
    shift = 1
    while shift < tokens:
        x = x + jnp.where(lane >= shift, pltpu.roll(x, shift, 1), 0.0)
        shift *= 2
    cum_ref[...] = x
    xt = jnp.concatenate([x, jnp.zeros((HD - PLANE, tokens), F32)], axis=0).T
    cumt_ref[...] = xt
    et = jnp.exp(xt)
    d = jnp.broadcast_to(jnp.exp(x[:, tokens - 1 : tokens]), (PLANE, HD))
    put_decays(d, heads, pay_ref, own_ref)
    for h in range(heads):
        s = slice(h * HD, (h + 1) * HD)
        f = slice((first + h) * HD, (first + h + 1) * HD)
        q = q_ref[:, f].astype(F32).astype(BF)
        qbf_ref[:, s] = q
        hi, lo = hi_lo(c_ref[:, f].astype(F32) * et[:, h : h + 1])
        both = dot(q, jnp.concatenate([hi, lo], axis=1), ((0,), (0,)))
        term = both[:, :HD] + both[:, HD:]
        own_ref[s, :] = term
        pay_ref[s, :] = term.astype(BF)


def state_terms(line, first, heads, q, c, ld):
    tokens = q.shape[0]
    rows = heads * HD + EXTRA
    outs = [((rows, HD), BF), ((rows, HD), F32), ((PLANE, tokens), F32), ((tokens, HD), F32)]
    outs.append(((tokens, heads * HD), BF))
    return line(functools.partial(state_kernel, first, heads), "state_terms", outs, [], [ld, q, c])


def put_decays(d, heads, pay_ref, own_ref):
    d_hi, d_mid = hi_lo(d)
    d_lo = (d - d_hi.astype(F32) - d_mid.astype(F32)).astype(BF)
    at = heads * HD
    pay_ref[at : at + PLANE, :] = d_hi
    pay_ref[at + PLANE : at + 2 * PLANE, :] = d_mid
    pay_ref[at + 2 * PLANE : at + EXTRA, :] = d_lo
    own_ref[at : at + PLANE, :] = d
    own_ref[at + PLANE : at + EXTRA, :] = jnp.zeros((EXTRA - PLANE, HD), F32)


def decays(ref, heads):
    p = ref[heads * HD :, :].astype(F32)
    return p[:PLANE] + p[PLANE : 2 * PLANE] + p[2 * PLANE :]


def append_kernel(heads, at, flags_ref, a_ref, b_ref, pay_ref, own_ref):
    swap = flags_ref[at] != 0
    da, db = decays(a_ref, heads), decays(b_ref, heads)
    one = jnp.ones_like(da)
    scale_a = jnp.where(swap, db, one)
    scale_b = jnp.where(swap, one, da)
    put_decays(da * db, heads, pay_ref, own_ref)
    for h in range(heads):
        s = slice(h * HD, (h + 1) * HD)
        term = scale_a[h : h + 1] * a_ref[s, :].astype(F32) + scale_b[h : h + 1] * b_ref[s, :].astype(F32)
        own_ref[s, :] = term
        pay_ref[s, :] = term.astype(BF)


def append(line, heads, flags, at, a, b):
    outs = [(a.shape, BF), (a.shape, F32)]
    return line(functools.partial(append_kernel, heads, at), "join_states", outs, [flags], [a, b])


def local_kernel(heads, cols, q_ref, k_ref, c_ref, cum_ref, cumt_ref, o_ref, kbf_ref):
    tokens = q_ref.shape[0]
    tile = 256
    row = lax.broadcasted_iota(jnp.int32, (tile, tile), 0)
    col = lax.broadcasted_iota(jnp.int32, (tile, tile), 1)
    causal = col >= row
    for h in range(heads):
        f = slice(cols + h * HD, cols + (h + 1) * HD)
        k = k_ref[:, f].astype(F32).astype(BF)
        kbf_ref[:, h * HD : (h + 1) * HD] = k
        scores = dot(k, q_ref[:, h * HD : (h + 1) * HD], ((1,), (1,)))
        strips = []
        for at in range(0, tokens, tile):
            end = at + tile
            before = cumt_ref[at:end, h : h + 1]
            gap = jnp.where(causal, cum_ref[h : h + 1, at:end] - before, -jnp.inf)
            strip = [jnp.zeros((tile, at), BF)] if at else []
            strip.append((scores[at:end, at:end] * jnp.exp(gap)).astype(BF))
            if end < tokens:
                middle = cum_ref[h : h + 1, end - 1 : end]
                to_t = jnp.exp(cum_ref[h : h + 1, end:] - middle)
                from_s = jnp.exp(middle - before)
                strip.append((scores[at:end, end:] * to_t * from_s).astype(BF))
            strips.append(jnp.concatenate(strip, axis=1))
        weighted = jnp.concatenate(strips, axis=0)
        o_ref[:, h * HD : (h + 1) * HD] = dot(weighted, c_ref[:, f], ((1,), (0,)))


def local_part(line, first, heads, q, k, c, cum, cumt):
    kernel = functools.partial(local_kernel, heads, first * HD)
    shape = (q.shape[0], heads * HD)
    return line(kernel, "local_part", [(shape, F32), (shape, BF)], [], [q, k, c, cum, cumt])


def value_kernel(heads, first, count, scale, flags_ref, k_ref, l_ref, cumt_ref, oth_ref, e_ref, r_ref, o_ref):
    tokens = k_ref.shape[0]
    is_first = flags_ref[0] == 0
    de = decays(e_ref, heads)
    do = decays(oth_ref, heads)
    use_oth = jnp.where(is_first, 1.0, 0.0)
    scale_e = jnp.where(is_first, do, jnp.ones_like(do))
    fall = jnp.exp(cumt_ref[tokens - 1 : tokens, :] - cumt_ref[...])
    for h in range(first, first + count):
        s = slice(h * HD, (h + 1) * HD)
        e = e_ref[s, :].astype(F32) + de[h : h + 1] * r_ref[s, :].astype(F32)
        carry = use_oth * oth_ref[s, :].astype(F32) + scale_e[h : h + 1] * e
        hi, lo = hi_lo(carry)
        both = dot(k_ref[:, s], jnp.concatenate([hi, lo], axis=1), ((1,), (0,)))
        carried = fall[:, h : h + 1] * (both[:, :HD] + both[:, HD:])
        at = (h - first) * HD
        o_ref[:, at : at + HD] = (scale * (l_ref[:, s] + carried)).astype(BF)


def value_grads(line, heads, first, count, scale, flags, arrays, after):
    kernel = functools.partial(value_kernel, heads, first, count, scale)
    outs = [((arrays[0].shape[0], count * HD), BF)]
    return line(kernel, "value_grad", outs, [flags], arrays, after)[0]


def input_kernel(rows, at, flags_ref, *refs):
    vs, w_ref, o_ref, v_all = refs[:-3], *refs[-3:]
    start = 0
    for v in vs:
        v_all[:, start : start + v.shape[1]] = v[...]
        start += v.shape[1]
    w = w_ref[pl.ds(pl.multiple_of(flags_ref[at] * rows, 128), rows), :]
    o_ref[...] = dot(v_all[...], w, ((1,), (1,))).astype(o_ref.dtype)


def input_part(line, flags, at, vs, w, rows, dtype, after=()):
    tokens, features = vs[0].shape[0], w.shape[1]
    scratch = [pltpu.VMEM((tokens, features), BF)]
    kernel = functools.partial(input_kernel, rows, at)
    return line(kernel, "input_part", [((tokens, rows), dtype)], [flags], [*vs, w], after, scratch)[0]


def last_input_kernel(total_ref, *refs):
    total = total_ref[...]
    for ref in refs[:-2]:
        total = total + ref[...].astype(F32)
    refs[-2][...] = total.astype(BF)
    refs[-1][...] = jnp.zeros_like(refs[-1])


def last_weight_kernel(scale, *refs):
    out = refs[-1]
    start = 0
    for keep, came in zip(refs[0:-1:2], refs[1:-1:2]):
        width = keep.shape[2]
        out[:, start : start + width] = scale * (keep[0] + came[0].astype(F32))
        start += width


def weight_kernel(sides, *refs):
    *pieces, v_ref, v_y_ref, away_ref, keep_ref = refs
    for s in range(sides):
        own, other = pieces[2 * s : 2 * s + 2]
        lows, _, rows, tokens = own.shape
        total = dot(own[...].reshape(-1, tokens), v_ref[...], ((1,), (0,)))
        total = total + dot(other[...].reshape(-1, tokens), v_y_ref[...], ((1,), (0,)))
        for low in range(lows):
            at = low * 2 * rows
            keep_ref[low * sides + s] = total[at : at + rows]
            away_ref[low * sides + s] = total[at + rows : at + 2 * rows].astype(BF)


def weight_part(line, pieces, vs, after):
    sides, (lows, _, rows, _) = len(pieces), pieces[0][0].shape
    shape = (lows * sides, rows, vs[0].shape[1])
    arrays = [p for side_pieces in pieces for p in side_pieces] + list(vs)
    kernel = functools.partial(weight_kernel, sides)
    return line(kernel, "weight_part", [(shape, BF), (shape, F32)], [], arrays, after, last=1)


def fold_kernel(at, start, flags_ref, keep_ref, came_ref, away_ref, left_ref):
    half, _, width = away_ref.shape
    cols = slice(start, start + width)
    kept = pl.ds(flags_ref[at] * half, half)
    sent = pl.ds((1 - flags_ref[at]) * half, half)
    left_ref[...] = keep_ref[kept, :, cols] + came_ref[kept, :, cols].astype(F32)
    away_ref[...] = (keep_ref[sent, :, cols] + came_ref[sent, :, cols].astype(F32)).astype(BF)


def fold(line, flags, at, keep, came, start=0, width=None):
    blocks, rows, all_columns = keep.shape
    shape = (blocks // 2, rows, width or all_columns)
    kernel = functools.partial(fold_kernel, at, start)
    return line(kernel, "fold_weight", [(shape, BF), (shape, F32)], [flags], [keep, came])


def tied(x, *after):
    return lax.optimization_barrier((x, *after))[0]


def swap_with(x, axis, bit):
    return lax.ppermute(x, axis, [(i, i ^ bit) for i in range(lax.axis_size(axis))])


def from_later(x, axis, shift):
    return lax.ppermute(x, axis, [(i, i - shift) for i in range(shift, lax.axis_size(axis))])


def local(inputs, value_weight, cotangent, spikes_q, spikes_k, log_decay):
    seqs, sides, dps = lax.axis_size("seq"), lax.axis_size("head"), lax.axis_size("dp")
    seq, side, dp = lax.axis_index("seq"), lax.axis_index("head"), lax.axis_index("dp")
    y, z = seq % 2, seq // 2
    tokens, rows_here = inputs.shape[1:]
    features = value_weight.shape[1]
    heads_here = log_decay.shape[1]
    seq_length = tokens * seqs
    grad_scale = 1.0 / (2.25 * HD * math.sqrt(seq_length))
    third = (heads_here + 2) // 4
    splits = [(third - 1,) * 2, (third, heads_here - 3 * third + 2)] if heads_here > 8 else [(third, heads_here - third)]
    sizes = [sum(split) for split in splits]
    starts = [sum(sizes[:g]) for g in range(len(sizes))]
    groups = len(sizes)
    rows = rows_here * sides // (seqs * dps)
    lows = rows_here // (2 * dps * rows)
    stages = (seqs // 2).bit_length() - 1

    q, k, c, ld = spikes_q[0], spikes_k[0], cotangent[0], log_decay[0]

    low_bits = lows.bit_length() - 1
    order = [int("0" + format(i, "b").zfill(low_bits)[::-1], 2) for i in range(lows)] if low_bits else [0]
    here = (z // lows) ^ side
    bits = list(range(low_bits)) + list(reversed(range(low_bits, stages)))

    at_sides = 4
    at_steps = at_sides + sides
    places = [y, dp, z % lows, jnp.zeros_like(y)] + [side ^ i for i in range(sides)]
    places += [(here >> max(b - low_bits, 0)) & int(b >= low_bits) for b in bits]
    flags = jnp.stack([p.astype(jnp.int32) for p in places])

    line = Line()
    own, other, joined, locals_, values, from_y = [], [], [], [], [], []

    def states(g):
        own.append(state_terms(line, starts[g], sizes[g], q, c, ld))
        other.append(swap_with(own[g][0], "seq", 1))

    def join(g):
        joined.append(append(line, sizes[g], flags, 0, own[g][1], other[g]))

    def spread(g):
        pay, ours = joined[g]
        e = None
        for stage in range(stages):
            later = from_later(pay, "seq", 2 << stage)
            if stage == 0:
                e = later
            elif stage < stages - 1:
                e = append(line, sizes[g], flags, 3, e, later)[1]
            if stage < stages - 1:
                pay, ours = append(line, sizes[g], flags, 3, ours, later)
        if stages == 1:
            later = jnp.zeros_like(later)
        joined[g] = (e, later)

    def local(g):
        _, _, cum, cumt, q_bf = own[g]
        locals_.append(local_part(line, starts[g], sizes[g], q_bf, k, c, cum, cumt))

    def value(g, *after):
        part, k_bf = locals_[g]
        arrays = [k_bf, part, own[g][3], other[g], *joined[g]]
        first = 0
        for count in splits[g]:
            v = value_grads(line, sizes[g], first, count, grad_scale, flags, arrays, after)
            values.append(v)
            from_y.append(swap_with(v, "seq", 1))
            first, after = first + count, ()

    kept, parts = {}, {}

    def matmul(i, *after):
        away, keep = weight_part(line, pieces, (values[i], from_y[i]), after)
        parts[i] = (keep, swap_with(away, "dp", 1))

    def over_dp(i, *widths):
        start = 0
        for j, width in enumerate(widths or [None]):
            away, keep = fold(line, flags, at_steps, *parts[i], start, width)
            kept[i, j] = (keep, swap_with(away, "seq", 2 << bits[0]))
            start += width or 0

    def over_z(i, j=0):
        for step, bit in enumerate(bits[1:], 1):
            away, keep = fold(line, flags, at_steps + step, *kept[i, j])
            kept[i, j] = (keep, swap_with(away, "seq", 2 << bit))

    others = []

    def input_others():
        for i in range(1, sides):
            part = input_part(line, flags, at_sides + i, values, value_weight, rows_here, BF)
            others.append(swap_with(part, "head", i))

    def input_own(*after):
        return input_part(line, flags, at_sides, values, value_weight, rows_here, F32, after)

    near, *far = transposed(line, flags, inputs[0], order, rows)
    near_x = [swap_with(near, "head", i) for i in range(1, sides)]
    for g in range(groups):
        states(g)
    far_x = [[] for _ in near_x]

    def send_far(i):
        piece = far[i]
        far[i] = swap_with(tied(piece, *line.last), "seq", 1)
        line.last.append(piece)

    def far_to_x(i):
        far[i] = line(copy_kernel, "pass_on", [(far[i].shape, BF)], [], [far[i]])[0]
        for j in range(1, sides):
            far_x[j - 1].append(swap_with(far[i], "head", j))

    join(0)
    send_far(0)
    if groups == 2:
        join(1)
    if len(far) == 2:
        send_far(1)
    local(0)
    spread(0)
    if groups == 2:
        local(1)
    for i in range(len(far)):
        far_to_x(i)
    value(0, *near_x)
    if groups == 2:
        spread(1)
    everything = [[p] for p in (near, *near_x)] + [far, *far_x]
    everything = merged(line, everything)
    pieces = list(zip(everything[:sides], everything[sides:]))
    if groups == 2:
        matmul(0)
        pause(line)
        over_dp(0)
        value(1)
        matmul(1)
        pause(line)
        over_dp(1)
        over_z(0)
        input_others()
        matmul(2)
        pause(line)
        over_dp(2)
        over_z(1)
        matmul(3)
        pause(line, [kept[0, 0][1]])
        over_dp(3, splits[1][1] // 2 * HD, (splits[1][1] + 1) // 2 * HD)
        over_z(2)
        over_z(3, 0)
        over_z(3, 1)
        total = input_own()
    else:
        matmul(0)
        matmul(1)
        over_dp(0)
        over_dp(1)
        over_z(0)
        input_others()
        total = input_own()
        over_z(1)
    outs = [(total.shape, BF), ((8, HD), F32)]
    grad_input = line(last_input_kernel, "grad_input", outs, [], [total, *others], last=1)[0]
    arrays = [a for i in sorted(kept) for a in kept[i]]
    kernel = functools.partial(last_weight_kernel, 1.0 / math.sqrt(dps * seq_length))
    grad_weight = line(kernel, "grad_weight", [((rows, features), F32)], [], arrays)[0]
    return grad_input[None], grad_weight


def solution(mesh):
    return jax.shard_map(
        local,
        mesh=mesh,
        in_specs=(
            P("dp", "seq", "head"),
            P(None, "head"),
            P("dp", "seq", "head"),
            P("dp", "seq", "head"),
            P("dp", "seq", "head"),
            P("dp", "head", "seq"),
        ),
        out_specs=(P("dp", "seq", "head"), P(("seq", "dp"), "head")),
        check_vma=False,
    )
```

```python
import functools
import math

import jax
import jax.numpy as jnp
from jax import lax
from jax.experimental import pallas as pl
from jax.experimental.pallas import tpu as pltpu
from jax.sharding import PartitionSpec as P

BF = jnp.bfloat16
F32 = jnp.float32
HD = 128
PLANE = 16
EXTRA = 3 * PLANE
PARAMS = pltpu.CompilerParams(vmem_limit_bytes=12 * 1024 * 1024)
VM = pl.BlockSpec(memory_space=pltpu.VMEM)
SM = pl.BlockSpec(memory_space=pltpu.SMEM)
ANY = pl.BlockSpec(memory_space=pl.ANY)


def dot(a, b, contract):
    return lax.dot_general(a, b, (contract, ((), ())), preferred_element_type=F32)


def hi_lo(x):
    hi = x.astype(BF)
    return hi, (x - hi.astype(F32)).astype(BF)


LONG = pl.CostEstimate(flops=2 * 10**10, transcendentals=0, bytes_accessed=0)


class Line:
    def __init__(self):
        self.last = []

    def __call__(self, kernel, name, outs, smalls, arrays, after=(), scratch=(), cost=LONG, last=0):
        waits = [*self.last, *after]
        first = len(smalls) + len(arrays)

        def body(*refs):
            kernel(*refs[:first], *refs[first + len(waits) :])

        results = pl.pallas_call(
            body,
            in_specs=[SM] * len(smalls) + [VM] * len(arrays) + [ANY] * len(waits),
            out_specs=[VM] * len(outs),
            out_shape=[jax.ShapeDtypeStruct(shape, dtype) for shape, dtype in outs],
            scratch_shapes=list(scratch),
            compiler_params=PARAMS,
            cost_estimate=cost,
            name=name,
        )(*smalls, *arrays, *waits)
        self.last = [results[last]]
        return results


def pause_kernel(o_ref):
    o_ref[...] = jnp.zeros_like(o_ref)


def pause(line, after=(), cost=LONG):
    line(pause_kernel, "pause", [((8, HD), F32)], [], [], after, (), cost)


def copy_kernel(*refs):
    outs = refs[len(refs) // 2 :]
    for ref, out in zip(refs, outs):
        out[...] = ref[...]


def merge_kernel(counts, *refs):
    first = 0
    for count, out in zip(counts, refs[sum(counts) :]):
        start = 0
        for ref in refs[first : first + count]:
            out[start : start + ref.shape[0]] = ref[...]
            start += ref.shape[0]
        first += count


def merged(line, groups):
    outs = [((sum(p.shape[0] for p in g), *g[0].shape[1:]), g[0].dtype) for g in groups]
    kernel = functools.partial(merge_kernel, [len(g) for g in groups])
    return line(kernel, "merge_inputs", outs, [], [p for g in groups for p in g])


def transpose_kernel(order, rows, at_ref, a_ref, near_ref, *refs):
    far_refs, flat = refs[:-1], refs[-1]
    flat[...] = a_ref[...].T.astype(flat.dtype)
    each = len(order) // len(far_refs)
    for yr in range(2):
        for dr in range(2):
            for i, low in enumerate(order):
                start = (((at_ref[2] ^ low) * 2 + (at_ref[0] ^ yr)) * 2 + (at_ref[1] ^ dr)) * rows
                piece = flat[pl.ds(pl.multiple_of(start, 8), rows), :].astype(BF)
                if yr == 0:
                    near_ref[i, dr] = piece
                else:
                    far_refs[i // each][i % each, dr] = piece


def transposed(line, at, a, order, rows):
    tokens, cols = a.shape
    halves = 2 if len(order) % 2 == 0 else 1
    outs = [((len(order), 2, rows, tokens), BF)] + [((len(order) // halves, 2, rows, tokens), BF)] * halves
    scratch = [pltpu.VMEM((cols, tokens), BF if rows % 16 == 0 else F32)]
    kernel = functools.partial(transpose_kernel, order, rows)
    return line(kernel, "transpose_inputs", outs, [at], [a], (), scratch)


def state_kernel(first, heads, flags_ref, ld_ref, q_ref, c_ref, pay_ref, own_ref, cum_ref, cumt_ref, qbf_ref):
    tokens = ld_ref.shape[1]
    half = (heads + 1) // 2
    y = flags_ref[0]
    x = ld_ref[first : first + heads, :]
    x = jnp.concatenate([x, jnp.zeros((PLANE - heads, tokens), F32)], axis=0)
    lane = lax.broadcasted_iota(jnp.int32, x.shape, 1)
    shift = 1
    while shift < tokens:
        x = x + jnp.where(lane >= shift, pltpu.roll(x, shift, 1), 0.0)
        shift *= 2
    cum_ref[...] = x
    xt = jnp.concatenate([x, jnp.zeros((HD - PLANE, tokens), F32)], axis=0).T
    cumt_ref[...] = xt
    et = jnp.exp(xt)
    d = jnp.broadcast_to(jnp.exp(x[:, tokens - 1 : tokens]), (PLANE, HD))
    later = jnp.concatenate([d[half:], d[:half]], axis=0)
    put_decays(jnp.where(y == 0, later, d), half, pay_ref, None)
    put_decays(jnp.where(y == 0, d, later), half, None, own_ref)

    def put_terms(low, high, at):
        s = slice(at * HD, (at + 1) * HD)
        own_ref[s, :] = jnp.where(y == 0, low, high)
        pay_ref[s, :] = jnp.where(y == 0, high, low).astype(BF)

    terms = []
    for h in range(heads):
        s = slice(h * HD, (h + 1) * HD)
        f = slice((first + h) * HD, (first + h + 1) * HD)
        q = q_ref[:, f].astype(F32).astype(BF)
        qbf_ref[:, s] = q
        hi, lo = hi_lo(c_ref[:, f].astype(F32) * et[:, h : h + 1])
        both = dot(q, jnp.concatenate([hi, lo], axis=1), ((0,), (0,)))
        terms.append(both[:, :HD] + both[:, HD:])
        if h >= half:
            put_terms(terms[h - half], terms[h], h - half)
    if heads % 2:
        put_terms(terms[half - 1], jnp.zeros((HD, HD), F32), half - 1)


def state_terms(line, first, heads, flags, q, c, ld):
    tokens = q.shape[0]
    rows = (heads + 1) // 2 * HD + EXTRA
    outs = [((rows, HD), BF), ((rows, HD), F32), ((PLANE, tokens), F32), ((tokens, HD), F32)]
    outs.append(((tokens, heads * HD), BF))
    return line(functools.partial(state_kernel, first, heads), "state_terms", outs, [flags], [ld, q, c])


def put_decays(d, heads, pay_ref, own_ref):
    at = heads * HD
    if pay_ref is not None:
        d_hi, d_mid = hi_lo(d)
        pay_ref[at : at + PLANE, :] = d_hi
        pay_ref[at + PLANE : at + 2 * PLANE, :] = d_mid
        pay_ref[at + 2 * PLANE : at + EXTRA, :] = (d - d_hi.astype(F32) - d_mid.astype(F32)).astype(BF)
    if own_ref is not None:
        own_ref[at : at + PLANE, :] = d
        own_ref[at + PLANE : at + EXTRA, :] = jnp.zeros((EXTRA - PLANE, HD), F32)


def decays(ref, heads):
    p = ref[heads * HD :, :].astype(F32)
    return p[:PLANE] + p[PLANE : 2 * PLANE] + p[2 * PLANE :]


def append_kernel(heads, at, flags_ref, a_ref, b_ref, pay_ref, own_ref):
    swap = flags_ref[at] != 0
    da, db = decays(a_ref, heads), decays(b_ref, heads)
    one = jnp.ones_like(da)
    scale_a = jnp.where(swap, db, one)
    scale_b = jnp.where(swap, one, da)
    put_decays(da * db, heads, pay_ref, own_ref)
    for h in range(heads):
        s = slice(h * HD, (h + 1) * HD)
        term = scale_a[h : h + 1] * a_ref[s, :].astype(F32) + scale_b[h : h + 1] * b_ref[s, :].astype(F32)
        own_ref[s, :] = term
        pay_ref[s, :] = term.astype(BF)


def append(line, heads, flags, at, a, b):
    outs = [(a.shape, BF), (a.shape, F32)]
    return line(functools.partial(append_kernel, heads, at), "join_states", outs, [flags], [a, b])


def local_kernel(heads, cols, q_ref, k_ref, c_ref, cum_ref, cumt_ref, o_ref, kbf_ref):
    tokens = q_ref.shape[0]
    tile = 256
    row = lax.broadcasted_iota(jnp.int32, (tile, tile), 0)
    col = lax.broadcasted_iota(jnp.int32, (tile, tile), 1)
    causal = col >= row
    for h in range(heads):
        f = slice(cols + h * HD, cols + (h + 1) * HD)
        k = k_ref[:, f].astype(F32).astype(BF)
        kbf_ref[:, h * HD : (h + 1) * HD] = k
        scores = dot(k, q_ref[:, h * HD : (h + 1) * HD], ((1,), (1,)))
        strips = []
        for at in range(0, tokens, tile):
            end = at + tile
            before = cumt_ref[at:end, h : h + 1]
            gap = jnp.where(causal, cum_ref[h : h + 1, at:end] - before, -jnp.inf)
            strip = [jnp.zeros((tile, at), BF)] if at else []
            strip.append((scores[at:end, at:end] * jnp.exp(gap)).astype(BF))
            if end < tokens:
                middle = cum_ref[h : h + 1, end - 1 : end]
                to_t = jnp.exp(cum_ref[h : h + 1, end:] - middle)
                from_s = jnp.exp(middle - before)
                strip.append((scores[at:end, end:] * to_t * from_s).astype(BF))
            strips.append(jnp.concatenate(strip, axis=1))
        weighted = jnp.concatenate(strips, axis=0)
        o_ref[:, h * HD : (h + 1) * HD] = dot(weighted, c_ref[:, f], ((1,), (0,)))


def local_part(line, first, heads, q, k, c, cum, cumt):
    kernel = functools.partial(local_kernel, heads, first * HD)
    shape = (q.shape[0], heads * HD)
    return line(kernel, "local_part", [(shape, F32), (shape, BF)], [], [q, k, c, cum, cumt])


def carry_kernel(heads, flags_ref, own_ref, oth_ref, e_ref, r_ref, theirs_ref, mine_ref):
    is_first = flags_ref[0] == 0
    de = decays(e_ref, heads)
    d_second = jnp.where(is_first, decays(oth_ref, heads), decays(own_ref, heads))
    for h in range(heads):
        s = slice(h * HD, (h + 1) * HD)
        second = e_ref[s, :].astype(F32) + de[h : h + 1] * r_ref[s, :].astype(F32)
        term = jnp.where(is_first, oth_ref[s, :].astype(F32), own_ref[s, :])
        first = term + d_second[h : h + 1] * second
        mine_ref[s, :] = jnp.where(is_first, first, second)
        theirs_ref[s, :] = jnp.where(is_first, second, first).astype(BF)


def carries(line, heads, flags, arrays):
    shape = (heads * HD, HD)
    kernel = functools.partial(carry_kernel, heads)
    return line(kernel, "carries", [(shape, BF), (shape, F32)], [flags], arrays)


def value_kernel(half, first, count, scale, flags_ref, k_ref, l_ref, cumt_ref, mine_ref, theirs_ref, o_ref):
    tokens = k_ref.shape[0]
    fall = jnp.exp(cumt_ref[tokens - 1 : tokens, :] - cumt_ref[...])
    for h in range(first, first + count):
        s = slice(h * HD, (h + 1) * HD)
        at = slice(h % half * HD, (h % half + 1) * HD)
        carry = jnp.where(flags_ref[0] == h // half, mine_ref[at, :], theirs_ref[at, :].astype(F32))
        hi, lo = hi_lo(carry)
        both = dot(k_ref[:, s], jnp.concatenate([hi, lo], axis=1), ((1,), (0,)))
        carried = fall[:, h : h + 1] * (both[:, :HD] + both[:, HD:])
        at = (h - first) * HD
        o_ref[:, at : at + HD] = (scale * (l_ref[:, s] + carried)).astype(BF)


def value_grads(line, half, first, count, scale, flags, arrays, after):
    kernel = functools.partial(value_kernel, half, first, count, scale)
    outs = [((arrays[0].shape[0], count * HD), BF)]
    return line(kernel, "value_grad", outs, [flags], arrays, after)[0]


def input_kernel(rows, at, first, count, flags_ref, *refs):
    *vs, w_ref, o_ref, v_all = refs[count:]
    start = 0
    for v in vs:
        v_all[:, start : start + v.shape[1]] = v[...]
        start += v.shape[1]
    cols = o_ref.shape[1] - first
    w = w_ref[pl.ds(pl.multiple_of(flags_ref[at] * rows + first, 128), cols), :]
    for before in refs[:count]:
        o_ref[:, :first] = before[...]
    o_ref[:, first:] = dot(v_all[...], w, ((1,), (1,))).astype(o_ref.dtype)


def input_part(line, flags, at, vs, w, rows, dtype, end, before=()):
    tokens, features = vs[0].shape[0], w.shape[1]
    first = before[0].shape[1] if before else 0
    scratch = [pltpu.VMEM((tokens, features), BF)]
    kernel = functools.partial(input_kernel, rows, at, first, len(before))
    outs = [((tokens, end), dtype)]
    return line(kernel, "input_part", outs, [flags], [*before, *vs, w], (), scratch)[0]


def last_input_kernel(total_ref, *refs):
    total = total_ref[...]
    for ref in refs[:-2]:
        total = total + ref[...].astype(F32)
    refs[-2][...] = total.astype(BF)
    refs[-1][...] = jnp.zeros_like(refs[-1])


def last_weight_kernel(scale, *refs):
    out = refs[-1]
    start = 0
    for keep, came in zip(refs[0:-1:2], refs[1:-1:2]):
        width = keep.shape[2]
        out[:, start : start + width] = scale * (keep[0] + came[0].astype(F32))
        start += width


def weight_kernel(sides, *refs):
    *pieces, v_ref, v_y_ref, away_ref, keep_ref = refs
    for s in range(sides):
        own, other = pieces[2 * s : 2 * s + 2]
        lows, _, rows, tokens = own.shape
        total = dot(own[...].reshape(-1, tokens), v_ref[...], ((1,), (0,)))
        total = total + dot(other[...].reshape(-1, tokens), v_y_ref[...], ((1,), (0,)))
        for low in range(lows):
            at = low * 2 * rows
            keep_ref[low * sides + s] = total[at : at + rows]
            away_ref[low * sides + s] = total[at + rows : at + 2 * rows].astype(BF)


def weight_part(line, pieces, vs, after):
    sides, (lows, _, rows, _) = len(pieces), pieces[0][0].shape
    shape = (lows * sides, rows, vs[0].shape[1])
    arrays = [p for side_pieces in pieces for p in side_pieces] + list(vs)
    kernel = functools.partial(weight_kernel, sides)
    return line(kernel, "weight_part", [(shape, BF), (shape, F32)], [], arrays, after, last=1)


def fold_kernel(at, start, flags_ref, keep_ref, came_ref, away_ref, left_ref):
    half, _, width = away_ref.shape
    cols = slice(start, start + width)
    kept = pl.ds(flags_ref[at] * half, half)
    sent = pl.ds((1 - flags_ref[at]) * half, half)
    left_ref[...] = keep_ref[kept, :, cols] + came_ref[kept, :, cols].astype(F32)
    away_ref[...] = (keep_ref[sent, :, cols] + came_ref[sent, :, cols].astype(F32)).astype(BF)


def fold(line, flags, at, keep, came, start=0, width=None):
    blocks, rows, all_columns = keep.shape
    shape = (blocks // 2, rows, width or all_columns)
    kernel = functools.partial(fold_kernel, at, start)
    return line(kernel, "fold_weight", [(shape, BF), (shape, F32)], [flags], [keep, came])


def tied(x, *after):
    return lax.optimization_barrier((x, *after))[0]


def swap_with(x, axis, bit):
    return lax.ppermute(x, axis, [(i, i ^ bit) for i in range(lax.axis_size(axis))])


def from_later(x, axis, shift):
    return lax.ppermute(x, axis, [(i, i - shift) for i in range(shift, lax.axis_size(axis))])


def local(inputs, value_weight, cotangent, spikes_q, spikes_k, log_decay):
    seqs, sides, dps = lax.axis_size("seq"), lax.axis_size("head"), lax.axis_size("dp")
    seq, side, dp = lax.axis_index("seq"), lax.axis_index("head"), lax.axis_index("dp")
    y, z = seq % 2, seq // 2
    tokens, rows_here = inputs.shape[1:]
    features = value_weight.shape[1]
    heads_here = log_decay.shape[1]
    seq_length = tokens * seqs
    grad_scale = 1.0 / (2.25 * HD * math.sqrt(seq_length))
    third = (heads_here + 2) // 4
    splits = [(third - 1,) * 2, (third, heads_here - 3 * third + 2)] if heads_here > 8 else [(third, heads_here - third)]
    sizes = [sum(split) for split in splits]
    starts = [sum(sizes[:g]) for g in range(len(sizes))]
    groups = len(sizes)
    rows = rows_here * sides // (seqs * dps)
    lows = rows_here // (2 * dps * rows)
    stages = (seqs // 2).bit_length() - 1

    q, k, c, ld = spikes_q[0], spikes_k[0], cotangent[0], log_decay[0]

    low_bits = lows.bit_length() - 1
    order = [int("0" + format(i, "b").zfill(low_bits)[::-1], 2) for i in range(lows)] if low_bits else [0]
    here = (z // lows) ^ side
    bits = list(range(low_bits)) + list(reversed(range(low_bits, stages)))

    at_sides = 4
    at_steps = at_sides + sides
    places = [y, dp, z % lows, jnp.zeros_like(y)] + [side ^ i for i in range(sides)]
    places += [(here >> max(b - low_bits, 0)) & int(b >= low_bits) for b in bits]
    flags = jnp.stack([p.astype(jnp.int32) for p in places])

    line = Line()
    own, other, joined, locals_, carried, values, from_y = [], [], [], [], [], [], []
    halves = [(size + 1) // 2 for size in sizes]

    def states(g):
        own.append(state_terms(line, starts[g], sizes[g], flags, q, c, ld))
        other.append(swap_with(own[g][0], "seq", 1))

    def join(g):
        joined.append(append(line, halves[g], flags, 0, own[g][1], other[g]))

    def spread(g):
        pay, ours = joined[g]
        e = None
        for stage in range(stages):
            later = from_later(pay, "seq", 2 << stage)
            if stage == 0:
                e = later
            elif stage < stages - 1:
                e = append(line, halves[g], flags, 3, e, later)[1]
            if stage < stages - 1:
                pay, ours = append(line, halves[g], flags, 3, ours, later)
        if stages == 1:
            later = jnp.zeros_like(later)
        joined[g] = (e, later)

    def carry(g):
        theirs, mine = carries(line, halves[g], flags, [own[g][1], other[g], *joined[g]])
        carried.append((mine, swap_with(theirs, "seq", 1)))

    def local(g):
        _, _, cum, cumt, q_bf = own[g]
        locals_.append(local_part(line, starts[g], sizes[g], q_bf, k, c, cum, cumt))

    def value(g, *after):
        part, k_bf = locals_[g]
        arrays = [k_bf, part, own[g][3], *carried[g]]
        first = 0
        for count in splits[g]:
            v = value_grads(line, halves[g], first, count, grad_scale, flags, arrays, after)
            values.append(v)
            from_y.append(swap_with(v, "seq", 1))
            first, after = first + count, ()

    kept, parts = {}, {}

    def matmul(i, *after):
        away, keep = weight_part(line, pieces, (values[i], from_y[i]), after)
        parts[i] = (keep, swap_with(away, "dp", 1))

    def over_dp(i, *widths):
        start = 0
        for j, width in enumerate(widths or [None]):
            away, keep = fold(line, flags, at_steps, *parts[i], start, width)
            kept[i, j] = (keep, swap_with(away, "seq", 2 << bits[0]))
            start += width or 0

    def over_z(i, j=0):
        for step, bit in enumerate(bits[1:], 1):
            away, keep = fold(line, flags, at_steps + step, *kept[i, j])
            kept[i, j] = (keep, swap_with(away, "seq", 2 << bit))

    others = []
    middle = rows_here // 2 if rows_here % 256 == 0 else 0

    def input_parts(at, dtype, step):
        if step == 0:
            if not middle:
                return pause(line)
            halves_done[at] = [input_part(line, flags, at, values, value_weight, rows_here, dtype, middle)]
        else:
            before = halves_done.get(at, ())
            return input_part(line, flags, at, values, value_weight, rows_here, dtype, rows_here, before)

    halves_done = {}

    def input_others(step):
        for i in range(1, sides):
            part = input_parts(at_sides + i, BF, step)
            if step:
                others.append(swap_with(part, "head", i))

    near, *far = transposed(line, flags, inputs[0], order, rows)
    near_x = [swap_with(near, "head", i) for i in range(1, sides)]
    for g in range(groups):
        states(g)
    far_x = [[] for _ in near_x]

    def send_far(i):
        piece = far[i]
        far[i] = swap_with(tied(piece, *line.last), "seq", 1)
        line.last.append(piece)

    def far_to_x(i):
        far[i] = line(copy_kernel, "pass_on", [(far[i].shape, BF)], [], [far[i]])[0]
        for j in range(1, sides):
            far_x[j - 1].append(swap_with(far[i], "head", j))

    join(0)
    send_far(0)
    if groups == 2:
        join(1)
    if len(far) == 2:
        send_far(1)
    local(0)
    spread(0)
    if groups == 2:
        local(1)
        spread(1)
    far_to_x(0)
    carry(0)
    if len(far) == 2:
        far_to_x(1)
    if groups == 2:
        carry(1)
    value(0, *near_x)
    if groups == 2:
        value(1, *[f[0] for f in far_x])
    everything = [[p] for p in (near, *near_x)] + [far, *far_x]
    everything = merged(line, everything)
    pieces = list(zip(everything[:sides], everything[sides:]))
    if groups == 2:
        matmul(0)
        input_others(0)
        over_dp(0)
        matmul(1)
        input_others(1)
        over_dp(1)
        over_z(0)
        matmul(2)
        input_parts(at_sides, F32, 0)
        over_dp(2)
        over_z(1)
        matmul(3)
        pause(line, [kept[0, 0][1]])
        over_dp(3, splits[1][1] // 2 * HD, (splits[1][1] + 1) // 2 * HD)
        over_z(2)
        pause(line)
        total = input_parts(at_sides, F32, 1)
        over_z(3, 0)
        over_z(3, 1)
    else:
        matmul(0)
        matmul(1)
        over_dp(0)
        over_dp(1)
        over_z(0)
        input_others(0)
        input_others(1)
        input_parts(at_sides, F32, 0)
        total = input_parts(at_sides, F32, 1)
        over_z(1)
    outs = [(total.shape, BF), ((8, HD), F32)]
    grad_input = line(last_input_kernel, "grad_input", outs, [], [total, *others], last=1)[0]
    arrays = [a for i in sorted(kept) for a in kept[i]]
    kernel = functools.partial(last_weight_kernel, 1.0 / math.sqrt(dps * seq_length))
    grad_weight = line(kernel, "grad_weight", [((rows, features), F32)], [], arrays)[0]
    return grad_input[None], grad_weight


def solution(mesh):
    return jax.shard_map(
        local,
        mesh=mesh,
        in_specs=(
            P("dp", "seq", "head"),
            P(None, "head"),
            P("dp", "seq", "head"),
            P("dp", "seq", "head"),
            P("dp", "seq", "head"),
            P("dp", "head", "seq"),
        ),
        out_specs=(P("dp", "seq", "head"), P(("seq", "dp"), "head")),
        check_vma=False,
    )
```

```python
import functools
import math

import jax
import jax.numpy as jnp
from jax import lax
from jax.experimental import pallas as pl
from jax.experimental.pallas import tpu as pltpu
from jax.sharding import PartitionSpec as P

BF = jnp.bfloat16
F32 = jnp.float32
HD = 128
PLANE = 16
EXTRA = 3 * PLANE
PARAMS = pltpu.CompilerParams(vmem_limit_bytes=6 * 1024 * 1024)
VM = pl.BlockSpec(memory_space=pltpu.VMEM)
SM = pl.BlockSpec(memory_space=pltpu.SMEM)
ANY = pl.BlockSpec(memory_space=pl.ANY)


def dot(a, b, contract):
    return lax.dot_general(a, b, (contract, ((), ())), preferred_element_type=F32)


def hi_lo(x):
    hi = x.astype(BF)
    return hi, (x - hi.astype(F32)).astype(BF)


LONG = pl.CostEstimate(flops=2 * 10**10, transcendentals=0, bytes_accessed=0)


class Line:
    def __init__(self):
        self.last = []

    def __call__(self, kernel, name, outs, smalls, arrays, after=(), scratch=(), cost=LONG, last=0):
        waits = [*self.last, *after]
        first = len(smalls) + len(arrays)

        def body(*refs):
            kernel(*refs[:first], *refs[first + len(waits) :])

        results = pl.pallas_call(
            body,
            in_specs=[SM] * len(smalls) + [VM] * len(arrays) + [ANY] * len(waits),
            out_specs=[VM] * len(outs),
            out_shape=[jax.ShapeDtypeStruct(shape, dtype) for shape, dtype in outs],
            scratch_shapes=list(scratch),
            compiler_params=PARAMS,
            cost_estimate=cost,
            name=name,
        )(*smalls, *arrays, *waits)
        self.last = [results[last]]
        return results


def pause_kernel(o_ref):
    o_ref[...] = jnp.zeros_like(o_ref)


def pause(line, after=(), cost=LONG):
    line(pause_kernel, "pause", [((8, HD), F32)], [], [], after, (), cost)


def copy_kernel(*refs):
    outs = refs[len(refs) // 2 :]
    for ref, out in zip(refs, outs):
        out[...] = ref[...]


def merge_kernel(counts, *refs):
    first = 0
    for count, out in zip(counts, refs[sum(counts) :]):
        start = 0
        for ref in refs[first : first + count]:
            out[start : start + ref.shape[0]] = ref[...]
            start += ref.shape[0]
        first += count


def merged(line, groups):
    outs = [((sum(p.shape[0] for p in g), *g[0].shape[1:]), g[0].dtype) for g in groups]
    kernel = functools.partial(merge_kernel, [len(g) for g in groups])
    return line(kernel, "merge_inputs", outs, [], [p for g in groups for p in g])


def transpose_kernel(order, rows, at_ref, a_ref, near_ref, *refs):
    far_refs, flat = refs[:-1], refs[-1]
    flat[...] = a_ref[...].T.astype(flat.dtype)
    each = len(order) // len(far_refs)
    for yr in range(2):
        for dr in range(2):
            for i, low in enumerate(order):
                start = (((at_ref[2] ^ low) * 2 + (at_ref[0] ^ yr)) * 2 + (at_ref[1] ^ dr)) * rows
                piece = flat[pl.ds(pl.multiple_of(start, 8), rows), :].astype(BF)
                if yr == 0:
                    near_ref[i, dr] = piece
                else:
                    far_refs[i // each][i % each, dr] = piece


def transposed(line, at, a, order, rows):
    tokens, cols = a.shape
    halves = 2 if len(order) % 2 == 0 else 1
    outs = [((len(order), 2, rows, tokens), BF)] + [((len(order) // halves, 2, rows, tokens), BF)] * halves
    scratch = [pltpu.VMEM((cols, tokens), BF if rows % 16 == 0 else F32)]
    kernel = functools.partial(transpose_kernel, order, rows)
    return line(kernel, "transpose_inputs", outs, [at], [a], (), scratch)


def state_kernel(first, heads, flags_ref, ld_ref, q_ref, c_ref, pay_ref, own_ref, cum_ref, cumt_ref, qbf_ref):
    tokens = ld_ref.shape[1]
    half = (heads + 1) // 2
    y = flags_ref[0]
    x = ld_ref[first : first + heads, :]
    x = jnp.concatenate([x, jnp.zeros((PLANE - heads, tokens), F32)], axis=0)
    lane = lax.broadcasted_iota(jnp.int32, x.shape, 1)
    shift = 1
    while shift < tokens:
        x = x + jnp.where(lane >= shift, pltpu.roll(x, shift, 1), 0.0)
        shift *= 2
    cum_ref[...] = x
    xt = jnp.concatenate([x, jnp.zeros((HD - PLANE, tokens), F32)], axis=0).T
    cumt_ref[...] = xt
    et = jnp.exp(xt)
    d = jnp.broadcast_to(jnp.exp(x[:, tokens - 1 : tokens]), (PLANE, HD))
    later = jnp.concatenate([d[half:], d[:half]], axis=0)
    put_decays(jnp.where(y == 0, later, d), half, pay_ref, None)
    put_decays(jnp.where(y == 0, d, later), half, None, own_ref)

    def put_terms(low, high, at):
        s = slice(at * HD, (at + 1) * HD)
        own_ref[s, :] = jnp.where(y == 0, low, high)
        pay_ref[s, :] = jnp.where(y == 0, high, low).astype(BF)

    terms = []
    for h in range(heads):
        s = slice(h * HD, (h + 1) * HD)
        f = slice((first + h) * HD, (first + h + 1) * HD)
        q = q_ref[:, f].astype(F32).astype(BF)
        qbf_ref[:, s] = q
        hi, lo = hi_lo(c_ref[:, f].astype(F32) * et[:, h : h + 1])
        both = dot(q, jnp.concatenate([hi, lo], axis=1), ((0,), (0,)))
        terms.append(both[:, :HD] + both[:, HD:])
        if h >= half:
            put_terms(terms[h - half], terms[h], h - half)
    if heads % 2:
        put_terms(terms[half - 1], jnp.zeros((HD, HD), F32), half - 1)


def state_terms(line, first, heads, flags, q, c, ld):
    tokens = q.shape[0]
    rows = (heads + 1) // 2 * HD + EXTRA
    outs = [((rows, HD), BF), ((rows, HD), F32), ((PLANE, tokens), F32), ((tokens, HD), F32)]
    outs.append(((tokens, heads * HD), BF))
    return line(functools.partial(state_kernel, first, heads), "state_terms", outs, [flags], [ld, q, c])


def put_decays(d, heads, pay_ref, own_ref):
    at = heads * HD
    if pay_ref is not None:
        d_hi, d_mid = hi_lo(d)
        pay_ref[at : at + PLANE, :] = d_hi
        pay_ref[at + PLANE : at + 2 * PLANE, :] = d_mid
        pay_ref[at + 2 * PLANE : at + EXTRA, :] = (d - d_hi.astype(F32) - d_mid.astype(F32)).astype(BF)
    if own_ref is not None:
        own_ref[at : at + PLANE, :] = d
        own_ref[at + PLANE : at + EXTRA, :] = jnp.zeros((EXTRA - PLANE, HD), F32)


def decays(ref, heads):
    p = ref[heads * HD :, :].astype(F32)
    return p[:PLANE] + p[PLANE : 2 * PLANE] + p[2 * PLANE :]


def append_kernel(heads, at, flags_ref, a_ref, b_ref, pay_ref, own_ref):
    swap = flags_ref[at] != 0
    da, db = decays(a_ref, heads), decays(b_ref, heads)
    one = jnp.ones_like(da)
    scale_a = jnp.where(swap, db, one)
    scale_b = jnp.where(swap, one, da)
    put_decays(da * db, heads, pay_ref, own_ref)
    for h in range(heads):
        s = slice(h * HD, (h + 1) * HD)
        term = scale_a[h : h + 1] * a_ref[s, :].astype(F32) + scale_b[h : h + 1] * b_ref[s, :].astype(F32)
        own_ref[s, :] = term
        pay_ref[s, :] = term.astype(BF)


def append(line, heads, flags, at, a, b):
    outs = [(a.shape, BF), (a.shape, F32)]
    return line(functools.partial(append_kernel, heads, at), "join_states", outs, [flags], [a, b])


def local_kernel(heads, cols, q_ref, k_ref, c_ref, cum_ref, cumt_ref, o_ref, kbf_ref):
    tokens = q_ref.shape[0]
    tile = 256
    row = lax.broadcasted_iota(jnp.int32, (tile, tile), 0)
    col = lax.broadcasted_iota(jnp.int32, (tile, tile), 1)
    causal = col >= row
    for h in range(heads):
        f = slice(cols + h * HD, cols + (h + 1) * HD)
        k = k_ref[:, f].astype(F32).astype(BF)
        kbf_ref[:, h * HD : (h + 1) * HD] = k
        scores = dot(k, q_ref[:, h * HD : (h + 1) * HD], ((1,), (1,)))
        strips = []
        for at in range(0, tokens, tile):
            end = at + tile
            before = cumt_ref[at:end, h : h + 1]
            gap = jnp.where(causal, cum_ref[h : h + 1, at:end] - before, -jnp.inf)
            strip = [jnp.zeros((tile, at), BF)] if at else []
            strip.append((scores[at:end, at:end] * jnp.exp(gap)).astype(BF))
            if end < tokens:
                middle = cum_ref[h : h + 1, end - 1 : end]
                to_t = jnp.exp(cum_ref[h : h + 1, end:] - middle)
                from_s = jnp.exp(middle - before)
                strip.append((scores[at:end, end:] * to_t * from_s).astype(BF))
            strips.append(jnp.concatenate(strip, axis=1))
        weighted = jnp.concatenate(strips, axis=0)
        o_ref[:, h * HD : (h + 1) * HD] = dot(weighted, c_ref[:, f], ((1,), (0,)))


def local_part(line, first, heads, q, k, c, cum, cumt):
    kernel = functools.partial(local_kernel, heads, first * HD)
    shape = (q.shape[0], heads * HD)
    return line(kernel, "local_part", [(shape, F32), (shape, BF)], [], [q, k, c, cum, cumt])


def carry_kernel(heads, flags_ref, own_ref, oth_ref, e_ref, r_ref, theirs_ref, mine_ref):
    is_first = flags_ref[0] == 0
    de = decays(e_ref, heads)
    d_second = jnp.where(is_first, decays(oth_ref, heads), decays(own_ref, heads))
    for h in range(heads):
        s = slice(h * HD, (h + 1) * HD)
        second = e_ref[s, :].astype(F32) + de[h : h + 1] * r_ref[s, :].astype(F32)
        term = jnp.where(is_first, oth_ref[s, :].astype(F32), own_ref[s, :])
        first = term + d_second[h : h + 1] * second
        mine_ref[s, :] = jnp.where(is_first, first, second)
        theirs_ref[s, :] = jnp.where(is_first, second, first).astype(BF)


def carries(line, heads, flags, arrays):
    shape = (heads * HD, HD)
    kernel = functools.partial(carry_kernel, heads)
    return line(kernel, "carries", [(shape, BF), (shape, F32)], [flags], arrays)


def value_kernel(half, first, count, scale, flags_ref, k_ref, l_ref, cumt_ref, mine_ref, theirs_ref, o_ref):
    tokens = k_ref.shape[0]
    fall = jnp.exp(cumt_ref[tokens - 1 : tokens, :] - cumt_ref[...])
    for h in range(first, first + count):
        s = slice(h * HD, (h + 1) * HD)
        at = slice(h % half * HD, (h % half + 1) * HD)
        carry = jnp.where(flags_ref[0] == h // half, mine_ref[at, :], theirs_ref[at, :].astype(F32))
        hi, lo = hi_lo(carry)
        both = dot(k_ref[:, s], jnp.concatenate([hi, lo], axis=1), ((1,), (0,)))
        carried = fall[:, h : h + 1] * (both[:, :HD] + both[:, HD:])
        at = (h - first) * HD
        o_ref[:, at : at + HD] = (scale * (l_ref[:, s] + carried)).astype(BF)


def value_grads(line, half, first, count, scale, flags, arrays, after):
    kernel = functools.partial(value_kernel, half, first, count, scale)
    outs = [((arrays[0].shape[0], count * HD), BF)]
    return line(kernel, "value_grad", outs, [flags], arrays, after)[0]


def join_and_input_kernel(rows, at, flags_ref, *refs):
    *vs, w_ref, o_ref, v_all = refs
    start = 0
    for v in vs:
        v_all[:, start : start + v.shape[1]] = v[...]
        start += v.shape[1]
    input_kernel(rows, at, 0, flags_ref, v_all, w_ref, o_ref)


def input_kernel(rows, at, first, flags_ref, *refs):
    *before, v_ref, w_ref, o_ref = refs
    for done in before:
        o_ref[:, :first] = done[...]
    cols = o_ref.shape[1] - first
    w = w_ref[pl.ds(pl.multiple_of(flags_ref[at] * rows + first, 128), cols), :]
    o_ref[:, first:] = dot(v_ref[...], w, ((1,), (1,))).astype(o_ref.dtype)


def first_input_part(line, flags, at, vs, w, rows, dtype, end):
    tokens, features = vs[0].shape[0], w.shape[1]
    outs = [((tokens, end), dtype), ((tokens, features), BF)]
    kernel = functools.partial(join_and_input_kernel, rows, at)
    return line(kernel, "input_part", outs, [flags], [*vs, w])


def input_part(line, flags, at, v, w, rows, dtype, end, before=()):
    first = before[0].shape[1] if before else 0
    kernel = functools.partial(input_kernel, rows, at, first)
    return line(kernel, "input_part", [((v.shape[0], end), dtype)], [flags], [*before, v, w])[0]


def last_input_kernel(total_ref, *refs):
    total = total_ref[...]
    for ref in refs[:-2]:
        total = total + ref[...].astype(F32)
    refs[-2][...] = total.astype(BF)
    refs[-1][...] = jnp.zeros_like(refs[-1])


def last_weight_kernel(scale, *refs):
    out = refs[-1]
    start = 0
    for keep, came in zip(refs[0:-1:2], refs[1:-1:2]):
        width = keep.shape[2]
        out[:, start : start + width] = scale * (keep[0] + came[0].astype(F32))
        start += width


def weight_kernel(sides, *refs):
    *pieces, v_ref, v_y_ref, away_ref, keep_ref = refs
    for s in range(sides):
        own, other = pieces[2 * s : 2 * s + 2]
        lows, _, rows, tokens = own.shape
        total = dot(own[...].reshape(-1, tokens), v_ref[...], ((1,), (0,)))
        total = total + dot(other[...].reshape(-1, tokens), v_y_ref[...], ((1,), (0,)))
        for low in range(lows):
            at = low * 2 * rows
            keep_ref[low * sides + s] = total[at : at + rows]
            away_ref[low * sides + s] = total[at + rows : at + 2 * rows].astype(BF)


def weight_part(line, pieces, vs, after):
    sides, (lows, _, rows, _) = len(pieces), pieces[0][0].shape
    shape = (lows * sides, rows, vs[0].shape[1])
    arrays = [p for side_pieces in pieces for p in side_pieces] + list(vs)
    kernel = functools.partial(weight_kernel, sides)
    return line(kernel, "weight_part", [(shape, BF), (shape, F32)], [], arrays, after, last=1)


def fold_kernel(at, start, flags_ref, keep_ref, came_ref, away_ref, left_ref):
    half, _, width = away_ref.shape
    cols = slice(start, start + width)
    kept = pl.ds(flags_ref[at] * half, half)
    sent = pl.ds((1 - flags_ref[at]) * half, half)
    left_ref[...] = keep_ref[kept, :, cols] + came_ref[kept, :, cols].astype(F32)
    away_ref[...] = (keep_ref[sent, :, cols] + came_ref[sent, :, cols].astype(F32)).astype(BF)


def fold(line, flags, at, keep, came, start=0, width=None):
    blocks, rows, all_columns = keep.shape
    shape = (blocks // 2, rows, width or all_columns)
    kernel = functools.partial(fold_kernel, at, start)
    return line(kernel, "fold_weight", [(shape, BF), (shape, F32)], [flags], [keep, came])


def tied(x, *after):
    return lax.optimization_barrier((x, *after))[0]


def swap_with(x, axis, bit):
    return lax.ppermute(x, axis, [(i, i ^ bit) for i in range(lax.axis_size(axis))])


def from_later(x, axis, shift):
    return lax.ppermute(x, axis, [(i, i - shift) for i in range(shift, lax.axis_size(axis))])


def local(inputs, value_weight, cotangent, spikes_q, spikes_k, log_decay):
    seqs, sides, dps = lax.axis_size("seq"), lax.axis_size("head"), lax.axis_size("dp")
    seq, side, dp = lax.axis_index("seq"), lax.axis_index("head"), lax.axis_index("dp")
    y, z = seq % 2, seq // 2
    tokens, rows_here = inputs.shape[1:]
    features = value_weight.shape[1]
    heads_here = log_decay.shape[1]
    seq_length = tokens * seqs
    grad_scale = 1.0 / (2.25 * HD * math.sqrt(seq_length))
    third = (heads_here + 2) // 4
    splits = [(third - 1,) * 2, (third, heads_here - 3 * third + 2)] if heads_here > 8 else [(third, heads_here - third)]
    sizes = [sum(split) for split in splits]
    starts = [sum(sizes[:g]) for g in range(len(sizes))]
    groups = len(sizes)
    rows = rows_here * sides // (seqs * dps)
    lows = rows_here // (2 * dps * rows)
    stages = (seqs // 2).bit_length() - 1

    q, k, c, ld = spikes_q[0], spikes_k[0], cotangent[0], log_decay[0]

    low_bits = lows.bit_length() - 1
    order = [int("0" + format(i, "b").zfill(low_bits)[::-1], 2) for i in range(lows)] if low_bits else [0]
    here = (z // lows) ^ side
    bits = list(range(low_bits)) + list(reversed(range(low_bits, stages)))

    at_sides = 4
    at_steps = at_sides + sides
    places = [y, dp, z % lows, jnp.zeros_like(y)] + [side ^ i for i in range(sides)]
    places += [(here >> max(b - low_bits, 0)) & int(b >= low_bits) for b in bits]
    flags = jnp.stack([p.astype(jnp.int32) for p in places])

    line = Line()
    own, other, joined, locals_, carried, values, from_y = [], [], [], [], [], [], []
    halves = [(size + 1) // 2 for size in sizes]

    def states(g):
        own.append(state_terms(line, starts[g], sizes[g], flags, q, c, ld))
        other.append(swap_with(own[g][0], "seq", 1))

    def join(g):
        joined.append(append(line, halves[g], flags, 0, own[g][1], other[g]))

    def spread(g):
        pay, ours = joined[g]
        e = None
        for stage in range(stages):
            later = from_later(pay, "seq", 2 << stage)
            if stage == 0:
                e = later
            elif stage < stages - 1:
                e = append(line, halves[g], flags, 3, e, later)[1]
            if stage < stages - 1:
                pay, ours = append(line, halves[g], flags, 3, ours, later)
        if stages == 1:
            later = jnp.zeros_like(later)
        joined[g] = (e, later)

    def carry(g):
        theirs, mine = carries(line, halves[g], flags, [own[g][1], other[g], *joined[g]])
        carried.append((mine, swap_with(theirs, "seq", 1)))

    def local(g):
        _, _, cum, cumt, q_bf = own[g]
        locals_.append(local_part(line, starts[g], sizes[g], q_bf, k, c, cum, cumt))

    def value(g, *after):
        part, k_bf = locals_[g]
        arrays = [k_bf, part, own[g][3], *carried[g]]
        first = 0
        for count in splits[g]:
            v = value_grads(line, halves[g], first, count, grad_scale, flags, arrays, after)
            values.append(v)
            from_y.append(swap_with(v, "seq", 1))
            first, after = first + count, ()

    kept, parts = {}, {}

    def matmul(i, *after):
        away, keep = weight_part(line, pieces, (values[i], from_y[i]), after)
        parts[i] = (keep, swap_with(away, "dp", 1))

    def over_dp(i, j=0, start=0, width=None):
        away, keep = fold(line, flags, at_steps, *parts[i], start, width)
        kept[i, j] = (keep, swap_with(away, "seq", 2 << bits[0]))

    def over_z(i, j=0):
        for step, bit in enumerate(bits[1:], 1):
            away, keep = fold(line, flags, at_steps + step, *kept[i, j])
            kept[i, j] = (keep, swap_with(away, "seq", 2 << bit))

    others = []
    middle = rows_here // 2 if rows_here % 256 == 0 else 0

    def input_parts(at, dtype, step):
        common = (value_weight, rows_here, dtype)
        if step == 0 and not middle:
            return pause(line)
        if step == 0 and not all_values:
            part, v = first_input_part(line, flags, at, values, *common, middle)
            all_values.append(v)
            halves_done[at] = [part]
        elif step == 0:
            halves_done[at] = [input_part(line, flags, at, all_values[0], *common, middle)]
        elif not all_values:
            part, v = first_input_part(line, flags, at, values, *common, rows_here)
            all_values.append(v)
            return part
        else:
            return input_part(line, flags, at, all_values[0], *common, rows_here, halves_done.get(at, ()))

    all_values = []
    halves_done = {}

    def input_others(step):
        for i in range(1, sides):
            part = input_parts(at_sides + i, BF, step)
            if step:
                others.append(swap_with(part, "head", i))

    near, *far = transposed(line, flags, inputs[0], order, rows)
    near_x = [swap_with(near, "head", i) for i in range(1, sides)]
    for g in range(groups):
        states(g)
    far_x = [[] for _ in near_x]

    def send_far(i):
        piece = far[i]
        far[i] = swap_with(tied(piece, *line.last), "seq", 1)
        line.last.append(piece)

    def far_to_x(i):
        far[i] = line(copy_kernel, "pass_on", [(far[i].shape, BF)], [], [far[i]])[0]
        for j in range(1, sides):
            far_x[j - 1].append(swap_with(far[i], "head", j))

    join(0)
    send_far(0)
    if groups == 2:
        join(1)
    if len(far) == 2:
        send_far(1)
    local(0)
    spread(0)
    if groups == 2:
        local(1)
        spread(1)
    far_to_x(0)
    carry(0)
    if len(far) == 2:
        far_to_x(1)
    if groups == 2:
        carry(1)
    value(0, *near_x)
    if groups == 2:
        value(1, *[f[0] for f in far_x])
    everything = [[p] for p in (near, *near_x)] + [far, *far_x]
    everything = merged(line, everything)
    pieces = list(zip(everything[:sides], everything[sides:]))
    if groups == 2:
        matmul(0)
        input_others(0)
        over_dp(0)
        matmul(1)
        input_others(1)
        over_dp(1)
        over_z(0)
        matmul(2)
        input_parts(at_sides, F32, 0)
        over_dp(2)
        matmul(3)
        pause(line, [kept[0, 0][1]])
        over_z(1)
        over_dp(3, 0, 0, splits[1][1] // 2 * HD)
        over_dp(3, 1, splits[1][1] // 2 * HD, (splits[1][1] + 1) // 2 * HD)
        over_z(2)
        over_z(3, 0)
        over_z(3, 1)
        total = input_parts(at_sides, F32, 1)
    else:
        matmul(0)
        matmul(1)
        over_dp(0)
        over_dp(1)
        over_z(0)
        input_others(0)
        input_others(1)
        input_parts(at_sides, F32, 0)
        total = input_parts(at_sides, F32, 1)
        over_z(1)
    outs = [(total.shape, BF), ((8, HD), F32)]
    grad_input = line(last_input_kernel, "grad_input", outs, [], [total, *others], last=1)[0]
    arrays = [a for i in sorted(kept) for a in kept[i]]
    kernel = functools.partial(last_weight_kernel, 1.0 / math.sqrt(dps * seq_length))
    grad_weight = line(kernel, "grad_weight", [((rows, features), F32)], [], arrays)[0]
    return grad_input[None], grad_weight


def solution(mesh):
    return jax.shard_map(
        local,
        mesh=mesh,
        in_specs=(
            P("dp", "seq", "head"),
            P(None, "head"),
            P("dp", "seq", "head"),
            P("dp", "seq", "head"),
            P("dp", "seq", "head"),
            P("dp", "head", "seq"),
        ),
        out_specs=(P("dp", "seq", "head"), P(("seq", "dp"), "head")),
        check_vma=False,
    )
```

```python
import functools
import math

import jax
import jax.numpy as jnp
from jax import lax
from jax.experimental import pallas as pl
from jax.experimental.pallas import tpu as pltpu
from jax.sharding import PartitionSpec as P

BF = jnp.bfloat16
F32 = jnp.float32
HD = 128
PLANE = 16
EXTRA = 3 * PLANE
PARAMS = pltpu.CompilerParams(vmem_limit_bytes=6 * 1024 * 1024)
VM = pl.BlockSpec(memory_space=pltpu.VMEM)
SM = pl.BlockSpec(memory_space=pltpu.SMEM)
ANY = pl.BlockSpec(memory_space=pl.ANY)


def dot(a, b, contract):
    return lax.dot_general(a, b, (contract, ((), ())), preferred_element_type=F32)


def hi_lo(x):
    hi = x.astype(BF)
    return hi, (x - hi.astype(F32)).astype(BF)


LONG = pl.CostEstimate(flops=2 * 10**10, transcendentals=0, bytes_accessed=0)


class Line:
    def __init__(self):
        self.last = []

    def __call__(self, kernel, name, outs, smalls, arrays, after=(), scratch=(), cost=LONG, last=0):
        waits = [*self.last, *after]
        first = len(smalls) + len(arrays)

        def body(*refs):
            kernel(*refs[:first], *refs[first + len(waits) :])

        results = pl.pallas_call(
            body,
            in_specs=[SM] * len(smalls) + [VM] * len(arrays) + [ANY] * len(waits),
            out_specs=[VM] * len(outs),
            out_shape=[jax.ShapeDtypeStruct(shape, dtype) for shape, dtype in outs],
            scratch_shapes=list(scratch),
            compiler_params=PARAMS,
            cost_estimate=cost,
            name=name,
        )(*smalls, *arrays, *waits)
        self.last = [results[last]]
        return results


def pause_kernel(o_ref):
    o_ref[...] = jnp.zeros_like(o_ref)


def pause(line, after=(), cost=LONG):
    line(pause_kernel, "pause", [((8, HD), F32)], [], [], after, (), cost)


def copy_kernel(*refs):
    outs = refs[len(refs) // 2 :]
    for ref, out in zip(refs, outs):
        out[...] = ref[...]


def merge_kernel(counts, *refs):
    first = 0
    for count, out in zip(counts, refs[sum(counts) :]):
        start = 0
        for ref in refs[first : first + count]:
            out[start : start + ref.shape[0]] = ref[...]
            start += ref.shape[0]
        first += count


def merged(line, groups):
    outs = [((sum(p.shape[0] for p in g), *g[0].shape[1:]), g[0].dtype) for g in groups]
    kernel = functools.partial(merge_kernel, [len(g) for g in groups])
    return line(kernel, "merge_inputs", outs, [], [p for g in groups for p in g])


def transpose_kernel(order, rows, at_ref, a_ref, near_ref, *refs):
    far_refs, flat = refs[:-1], refs[-1]
    flat[...] = a_ref[...].T.astype(flat.dtype)
    each = len(order) // len(far_refs)
    for yr in range(2):
        for dr in range(2):
            for i, low in enumerate(order):
                start = (((at_ref[2] ^ low) * 2 + (at_ref[0] ^ yr)) * 2 + (at_ref[1] ^ dr)) * rows
                piece = flat[pl.ds(pl.multiple_of(start, 8), rows), :].astype(BF)
                if yr == 0:
                    near_ref[i, dr] = piece
                else:
                    far_refs[i // each][i % each, dr] = piece


def transposed(line, at, a, order, rows):
    tokens, cols = a.shape
    halves = 2 if len(order) % 2 == 0 else 1
    outs = [((len(order), 2, rows, tokens), BF)] + [((len(order) // halves, 2, rows, tokens), BF)] * halves
    scratch = [pltpu.VMEM((cols, tokens), BF if rows % 16 == 0 else F32)]
    kernel = functools.partial(transpose_kernel, order, rows)
    return line(kernel, "transpose_inputs", outs, [at], [a], (), scratch)


def state_kernel(first, heads, flags_ref, ld_ref, q_ref, c_ref, pay_ref, own_ref, cum_ref, cumt_ref, qbf_ref):
    tokens = ld_ref.shape[1]
    half = (heads + 1) // 2
    y = flags_ref[0]
    x = ld_ref[first : first + heads, :]
    x = jnp.concatenate([x, jnp.zeros((PLANE - heads, tokens), F32)], axis=0)
    lane = lax.broadcasted_iota(jnp.int32, x.shape, 1)
    shift = 1
    while shift < tokens:
        x = x + jnp.where(lane >= shift, pltpu.roll(x, shift, 1), 0.0)
        shift *= 2
    cum_ref[...] = x
    xt = jnp.concatenate([x, jnp.zeros((HD - PLANE, tokens), F32)], axis=0).T
    cumt_ref[...] = xt
    et = jnp.exp(xt)
    d = jnp.broadcast_to(jnp.exp(x[:, tokens - 1 : tokens]), (PLANE, HD))
    later = jnp.concatenate([d[half:], d[:half]], axis=0)
    put_decays(jnp.where(y == 0, later, d), half, pay_ref, None)
    put_decays(jnp.where(y == 0, d, later), half, None, own_ref)

    def put_terms(low, high, at):
        s = slice(at * HD, (at + 1) * HD)
        own_ref[s, :] = jnp.where(y == 0, low, high)
        pay_ref[s, :] = jnp.where(y == 0, high, low).astype(BF)

    terms = []
    for h in range(heads):
        s = slice(h * HD, (h + 1) * HD)
        f = slice((first + h) * HD, (first + h + 1) * HD)
        q = q_ref[:, f].astype(F32).astype(BF)
        qbf_ref[:, s] = q
        hi, lo = hi_lo(c_ref[:, f].astype(F32) * et[:, h : h + 1])
        both = dot(q, jnp.concatenate([hi, lo], axis=1), ((0,), (0,)))
        terms.append(both[:, :HD] + both[:, HD:])
        if h >= half:
            put_terms(terms[h - half], terms[h], h - half)
    if heads % 2:
        put_terms(terms[half - 1], jnp.zeros((HD, HD), F32), half - 1)


def state_terms(line, first, heads, flags, q, c, ld):
    tokens = q.shape[0]
    rows = (heads + 1) // 2 * HD + EXTRA
    outs = [((rows, HD), BF), ((rows, HD), F32), ((PLANE, tokens), F32), ((tokens, HD), F32)]
    outs.append(((tokens, heads * HD), BF))
    return line(functools.partial(state_kernel, first, heads), "state_terms", outs, [flags], [ld, q, c])


def put_decays(d, heads, pay_ref, own_ref):
    at = heads * HD
    if pay_ref is not None:
        d_hi, d_mid = hi_lo(d)
        pay_ref[at : at + PLANE, :] = d_hi
        pay_ref[at + PLANE : at + 2 * PLANE, :] = d_mid
        pay_ref[at + 2 * PLANE : at + EXTRA, :] = (d - d_hi.astype(F32) - d_mid.astype(F32)).astype(BF)
    if own_ref is not None:
        own_ref[at : at + PLANE, :] = d
        own_ref[at + PLANE : at + EXTRA, :] = jnp.zeros((EXTRA - PLANE, HD), F32)


def decays(ref, heads):
    p = ref[heads * HD :, :].astype(F32)
    return p[:PLANE] + p[PLANE : 2 * PLANE] + p[2 * PLANE :]


def append_kernel(heads, at, flags_ref, a_ref, b_ref, pay_ref, own_ref):
    swap = flags_ref[at] != 0
    da, db = decays(a_ref, heads), decays(b_ref, heads)
    one = jnp.ones_like(da)
    scale_a = jnp.where(swap, db, one)
    scale_b = jnp.where(swap, one, da)
    put_decays(da * db, heads, pay_ref, own_ref)
    for h in range(heads):
        s = slice(h * HD, (h + 1) * HD)
        term = scale_a[h : h + 1] * a_ref[s, :].astype(F32) + scale_b[h : h + 1] * b_ref[s, :].astype(F32)
        own_ref[s, :] = term
        pay_ref[s, :] = term.astype(BF)


def append(line, heads, flags, at, a, b):
    outs = [(a.shape, BF), (a.shape, F32)]
    return line(functools.partial(append_kernel, heads, at), "join_states", outs, [flags], [a, b])


def local_kernel(heads, cols, q_ref, k_ref, c_ref, cum_ref, cumt_ref, o_ref, kbf_ref):
    tokens = q_ref.shape[0]
    tile = 256
    row = lax.broadcasted_iota(jnp.int32, (tile, tile), 0)
    col = lax.broadcasted_iota(jnp.int32, (tile, tile), 1)
    causal = col >= row
    for h in range(heads):
        f = slice(cols + h * HD, cols + (h + 1) * HD)
        k = k_ref[:, f].astype(F32).astype(BF)
        kbf_ref[:, h * HD : (h + 1) * HD] = k
        scores = dot(k, q_ref[:, h * HD : (h + 1) * HD], ((1,), (1,)))
        strips = []
        for at in range(0, tokens, tile):
            end = at + tile
            before = cumt_ref[at:end, h : h + 1]
            gap = jnp.where(causal, cum_ref[h : h + 1, at:end] - before, -jnp.inf)
            strip = [jnp.zeros((tile, at), BF)] if at else []
            strip.append((scores[at:end, at:end] * jnp.exp(gap)).astype(BF))
            if end < tokens:
                middle = cum_ref[h : h + 1, end - 1 : end]
                to_t = jnp.exp(cum_ref[h : h + 1, end:] - middle)
                from_s = jnp.exp(middle - before)
                strip.append((scores[at:end, end:] * to_t * from_s).astype(BF))
            strips.append(jnp.concatenate(strip, axis=1))
        weighted = jnp.concatenate(strips, axis=0)
        o_ref[:, h * HD : (h + 1) * HD] = dot(weighted, c_ref[:, f], ((1,), (0,)))


def local_part(line, first, heads, q, k, c, cum, cumt):
    kernel = functools.partial(local_kernel, heads, first * HD)
    shape = (q.shape[0], heads * HD)
    return line(kernel, "local_part", [(shape, F32), (shape, BF)], [], [q, k, c, cum, cumt])


def carry_kernel(heads, flags_ref, own_ref, oth_ref, e_ref, r_ref, theirs_ref, mine_ref):
    is_first = flags_ref[0] == 0
    de = decays(e_ref, heads)
    d_second = jnp.where(is_first, decays(oth_ref, heads), decays(own_ref, heads))
    for h in range(heads):
        s = slice(h * HD, (h + 1) * HD)
        second = e_ref[s, :].astype(F32) + de[h : h + 1] * r_ref[s, :].astype(F32)
        term = jnp.where(is_first, oth_ref[s, :].astype(F32), own_ref[s, :])
        first = term + d_second[h : h + 1] * second
        mine_ref[s, :] = jnp.where(is_first, first, second)
        theirs_ref[s, :] = jnp.where(is_first, second, first).astype(BF)


def carries(line, heads, flags, arrays):
    shape = (heads * HD, HD)
    kernel = functools.partial(carry_kernel, heads)
    return line(kernel, "carries", [(shape, BF), (shape, F32)], [flags], arrays)


def value_kernel(half, first, count, scale, flags_ref, k_ref, l_ref, cumt_ref, mine_ref, theirs_ref, o_ref):
    tokens = k_ref.shape[0]
    fall = jnp.exp(cumt_ref[tokens - 1 : tokens, :] - cumt_ref[...])
    for h in range(first, first + count):
        s = slice(h * HD, (h + 1) * HD)
        at = slice(h % half * HD, (h % half + 1) * HD)
        carry = jnp.where(flags_ref[0] == h // half, mine_ref[at, :], theirs_ref[at, :].astype(F32))
        hi, lo = hi_lo(carry)
        both = dot(k_ref[:, s], jnp.concatenate([hi, lo], axis=1), ((1,), (0,)))
        carried = fall[:, h : h + 1] * (both[:, :HD] + both[:, HD:])
        at = (h - first) * HD
        o_ref[:, at : at + HD] = (scale * (l_ref[:, s] + carried)).astype(BF)


def value_grads(line, half, first, count, scale, flags, arrays, after):
    kernel = functools.partial(value_kernel, half, first, count, scale)
    outs = [((arrays[0].shape[0], count * HD), BF)]
    return line(kernel, "value_grad", outs, [flags], arrays, after)[0]


def join_and_input_kernel(rows, at, flags_ref, *refs):
    *vs, w_ref, o_ref, v_all = refs
    start = 0
    for v in vs:
        v_all[:, start : start + v.shape[1]] = v[...]
        start += v.shape[1]
    input_kernel(rows, at, 0, flags_ref, v_all, w_ref, o_ref)


def input_kernel(rows, at, first, flags_ref, *refs):
    *before, v_ref, w_ref, o_ref = refs
    for done in before:
        o_ref[:, :first] = done[...]
    cols = o_ref.shape[1] - first
    w = w_ref[pl.ds(pl.multiple_of(flags_ref[at] * rows + first, 128), cols), :]
    o_ref[:, first:] = dot(v_ref[...], w, ((1,), (1,))).astype(o_ref.dtype)


def first_input_part(line, flags, at, vs, w, rows, dtype, end):
    tokens, features = vs[0].shape[0], w.shape[1]
    outs = [((tokens, end), dtype), ((tokens, features), BF)]
    kernel = functools.partial(join_and_input_kernel, rows, at)
    return line(kernel, "input_part", outs, [flags], [*vs, w])


def input_part(line, flags, at, v, w, rows, dtype, end, before=()):
    first = before[0].shape[1] if before else 0
    kernel = functools.partial(input_kernel, rows, at, first)
    return line(kernel, "input_part", [((v.shape[0], end), dtype)], [flags], [*before, v, w])[0]


def last_input_kernel(total_ref, *refs):
    total = total_ref[...]
    for ref in refs[:-2]:
        total = total + ref[...].astype(F32)
    refs[-2][...] = total.astype(BF)
    refs[-1][...] = jnp.zeros_like(refs[-1])


def last_weight_kernel(scale, *refs):
    out = refs[-1]
    start = 0
    for keep, came in zip(refs[0:-1:2], refs[1:-1:2]):
        width = keep.shape[2]
        out[:, start : start + width] = scale * (keep[0] + came[0].astype(F32))
        start += width


def weight_kernel(sides, *refs):
    *pieces, v_ref, v_y_ref, away_ref, keep_ref = refs
    for s in range(sides):
        own, other = pieces[2 * s : 2 * s + 2]
        lows, _, rows, tokens = own.shape
        total = dot(own[...].reshape(-1, tokens), v_ref[...], ((1,), (0,)))
        total = total + dot(other[...].reshape(-1, tokens), v_y_ref[...], ((1,), (0,)))
        for low in range(lows):
            at = low * 2 * rows
            keep_ref[low * sides + s] = total[at : at + rows]
            away_ref[low * sides + s] = total[at + rows : at + 2 * rows].astype(BF)


def weight_part(line, pieces, vs, after):
    sides, (lows, _, rows, _) = len(pieces), pieces[0][0].shape
    shape = (lows * sides, rows, vs[0].shape[1])
    arrays = [p for side_pieces in pieces for p in side_pieces] + list(vs)
    kernel = functools.partial(weight_kernel, sides)
    return line(kernel, "weight_part", [(shape, BF), (shape, F32)], [], arrays, after, last=1)


def fold_kernel(at, start, flags_ref, keep_ref, came_ref, away_ref, left_ref):
    half, _, width = away_ref.shape
    cols = slice(start, start + width)
    kept = pl.ds(flags_ref[at] * half, half)
    sent = pl.ds((1 - flags_ref[at]) * half, half)
    left_ref[...] = keep_ref[kept, :, cols] + came_ref[kept, :, cols].astype(F32)
    away_ref[...] = (keep_ref[sent, :, cols] + came_ref[sent, :, cols].astype(F32)).astype(BF)


def fold(line, flags, at, keep, came, start=0, width=None):
    blocks, rows, all_columns = keep.shape
    shape = (blocks // 2, rows, width or all_columns)
    kernel = functools.partial(fold_kernel, at, start)
    return line(kernel, "fold_weight", [(shape, BF), (shape, F32)], [flags], [keep, came])


def tied(x, *after):
    return lax.optimization_barrier((x, *after))[0]


def swap_with(x, axis, bit):
    return lax.ppermute(x, axis, [(i, i ^ bit) for i in range(lax.axis_size(axis))])


def from_later(x, axis, shift):
    return lax.ppermute(x, axis, [(i, i - shift) for i in range(shift, lax.axis_size(axis))])


def local(inputs, value_weight, cotangent, spikes_q, spikes_k, log_decay):
    seqs, sides, dps = lax.axis_size("seq"), lax.axis_size("head"), lax.axis_size("dp")
    seq, side, dp = lax.axis_index("seq"), lax.axis_index("head"), lax.axis_index("dp")
    y, z = seq % 2, seq // 2
    tokens, rows_here = inputs.shape[1:]
    features = value_weight.shape[1]
    heads_here = log_decay.shape[1]
    seq_length = tokens * seqs
    grad_scale = 1.0 / (2.25 * HD * math.sqrt(seq_length))
    third = (heads_here + 2) // 4
    splits = [(third - 1,) * 2, (third, heads_here - 3 * third + 2)] if heads_here > 8 else [(third, heads_here - third)]
    sizes = [sum(split) for split in splits]
    starts = [sum(sizes[:g]) for g in range(len(sizes))]
    groups = len(sizes)
    rows = rows_here * sides // (seqs * dps)
    lows = rows_here // (2 * dps * rows)
    stages = (seqs // 2).bit_length() - 1

    q, k, c, ld = spikes_q[0], spikes_k[0], cotangent[0], log_decay[0]

    low_bits = lows.bit_length() - 1
    order = [int("0" + format(i, "b").zfill(low_bits)[::-1], 2) for i in range(lows)] if low_bits else [0]
    here = (z // lows) ^ side
    bits = list(range(low_bits)) + list(reversed(range(low_bits, stages)))

    at_sides = 4
    at_steps = at_sides + sides
    places = [y, dp, z % lows, jnp.zeros_like(y)] + [side ^ i for i in range(sides)]
    places += [(here >> max(b - low_bits, 0)) & int(b >= low_bits) for b in bits]
    flags = jnp.stack([p.astype(jnp.int32) for p in places])

    line = Line()
    own, other, joined, locals_, carried, values, from_y = [], [], [], [], [], [], []
    halves = [(size + 1) // 2 for size in sizes]

    def states(g):
        own.append(state_terms(line, starts[g], sizes[g], flags, q, c, ld))
        other.append(swap_with(own[g][0], "seq", 1))

    def join(g):
        joined.append(append(line, halves[g], flags, 0, own[g][1], other[g]))

    def spread(g):
        pay, ours = joined[g]
        e = None
        for stage in range(stages):
            later = from_later(pay, "seq", 2 << stage)
            if stage == 0:
                e = later
            elif stage < stages - 1:
                e = append(line, halves[g], flags, 3, e, later)[1]
            if stage < stages - 1:
                pay, ours = append(line, halves[g], flags, 3, ours, later)
        if stages == 1:
            later = jnp.zeros_like(later)
        joined[g] = (e, later)

    def carry(g):
        theirs, mine = carries(line, halves[g], flags, [own[g][1], other[g], *joined[g]])
        carried.append((mine, swap_with(theirs, "seq", 1)))

    def local(g):
        _, _, cum, cumt, q_bf = own[g]
        locals_.append(local_part(line, starts[g], sizes[g], q_bf, k, c, cum, cumt))

    def value(g, *after):
        part, k_bf = locals_[g]
        arrays = [k_bf, part, own[g][3], *carried[g]]
        first = 0
        for count in splits[g]:
            v = value_grads(line, halves[g], first, count, grad_scale, flags, arrays, after)
            values.append(v)
            from_y.append(swap_with(v, "seq", 1))
            first, after = first + count, ()

    kept, parts = {}, {}

    def matmul(i, *after):
        away, keep = weight_part(line, pieces, (values[i], from_y[i]), after)
        parts[i] = (keep, swap_with(away, "dp", 1))

    def over_dp(i, j=0, start=0, width=None):
        away, keep = fold(line, flags, at_steps, *parts[i], start, width)
        kept[i, j] = (keep, swap_with(away, "seq", 2 << bits[0]))

    def over_z(i, j=0):
        for step, bit in enumerate(bits[1:], 1):
            away, keep = fold(line, flags, at_steps + step, *kept[i, j])
            kept[i, j] = (keep, swap_with(away, "seq", 2 << bit))

    others = []
    middle = rows_here // 2 if rows_here % 256 == 0 else 0

    def input_parts(at, dtype, step):
        common = (value_weight, rows_here, dtype)
        if step == 0 and not middle:
            return pause(line)
        if step == 0 and not all_values:
            part, v = first_input_part(line, flags, at, values, *common, middle)
            all_values.append(v)
            halves_done[at] = [part]
        elif step == 0:
            halves_done[at] = [input_part(line, flags, at, all_values[0], *common, middle)]
        elif not all_values:
            part, v = first_input_part(line, flags, at, values, *common, rows_here)
            all_values.append(v)
            return part
        else:
            return input_part(line, flags, at, all_values[0], *common, rows_here, halves_done.get(at, ()))

    all_values = []
    halves_done = {}

    def input_others(step):
        for i in range(1, sides):
            part = input_parts(at_sides + i, BF, step)
            if step:
                others.append(swap_with(part, "head", i))

    near, *far = transposed(line, flags, inputs[0], order, rows)
    near_x = [swap_with(near, "head", i) for i in range(1, sides)]
    for g in range(groups):
        states(g)
    far_x = [[] for _ in near_x]

    def send_far(i):
        piece = far[i]
        far[i] = swap_with(tied(piece, *line.last), "seq", 1)
        line.last.append(piece)

    def far_to_x(i):
        far[i] = line(copy_kernel, "pass_on", [(far[i].shape, BF)], [], [far[i]])[0]
        for j in range(1, sides):
            far_x[j - 1].append(swap_with(far[i], "head", j))

    send_far(0)
    join(0)
    if len(far) == 2:
        send_far(1)
    if groups == 2:
        join(1)
    local(0)
    spread(0)
    if groups == 2:
        local(1)
        spread(1)
    far_to_x(0)
    carry(0)
    if len(far) == 2:
        far_to_x(1)
    if groups == 2:
        carry(1)
    value(0, *near_x)
    if groups == 2:
        value(1, *[f[0] for f in far_x])
    everything = [[p] for p in (near, *near_x)] + [far, *far_x]
    everything = merged(line, everything)
    pieces = list(zip(everything[:sides], everything[sides:]))
    if groups == 2:
        matmul(0)
        input_others(0)
        over_dp(0)
        matmul(1)
        input_others(1)
        over_dp(1)
        over_z(0)
        matmul(2)
        input_parts(at_sides, F32, 0)
        over_dp(2)
        matmul(3)
        pause(line, [kept[0, 0][1]])
        over_z(1)
        over_dp(3, 0, 0, splits[1][1] // 2 * HD)
        over_dp(3, 1, splits[1][1] // 2 * HD, (splits[1][1] + 1) // 2 * HD)
        over_z(2)
        over_z(3, 0)
        over_z(3, 1)
        total = input_parts(at_sides, F32, 1)
    else:
        matmul(0)
        matmul(1)
        over_dp(0)
        over_dp(1)
        over_z(0)
        input_others(0)
        input_others(1)
        input_parts(at_sides, F32, 0)
        total = input_parts(at_sides, F32, 1)
        over_z(1)
    outs = [(total.shape, BF), ((8, HD), F32)]
    grad_input = line(last_input_kernel, "grad_input", outs, [], [total, *others], last=1)[0]
    arrays = [a for i in sorted(kept) for a in kept[i]]
    kernel = functools.partial(last_weight_kernel, 1.0 / math.sqrt(dps * seq_length))
    grad_weight = line(kernel, "grad_weight", [((rows, features), F32)], [], arrays)[0]
    return grad_input[None], grad_weight


def solution(mesh):
    return jax.shard_map(
        local,
        mesh=mesh,
        in_specs=(
            P("dp", "seq", "head"),
            P(None, "head"),
            P("dp", "seq", "head"),
            P("dp", "seq", "head"),
            P("dp", "seq", "head"),
            P("dp", "head", "seq"),
        ),
        out_specs=(P("dp", "seq", "head"), P(("seq", "dp"), "head")),
        check_vma=False,
    )
```

```python
import functools
import math

import jax
import jax.numpy as jnp
from jax import lax
from jax.experimental import pallas as pl
from jax.experimental.pallas import tpu as pltpu
from jax.sharding import PartitionSpec as P

BF = jnp.bfloat16
F32 = jnp.float32
HD = 128
PLANE = 16
EXTRA = 3 * PLANE
PARAMS = pltpu.CompilerParams(vmem_limit_bytes=6 * 1024 * 1024)
VM = pl.BlockSpec(memory_space=pltpu.VMEM)
SM = pl.BlockSpec(memory_space=pltpu.SMEM)
ANY = pl.BlockSpec(memory_space=pl.ANY)


def dot(a, b, contract):
    return lax.dot_general(a, b, (contract, ((), ())), preferred_element_type=F32)


def hi_lo(x):
    hi = x.astype(BF)
    return hi, (x - hi.astype(F32)).astype(BF)


LONG = pl.CostEstimate(flops=2 * 10**10, transcendentals=0, bytes_accessed=0)


class Line:
    def __init__(self):
        self.last = []

    def __call__(self, kernel, name, outs, smalls, arrays, after=(), scratch=(), cost=LONG, last=0):
        waits = [*self.last, *after]
        first = len(smalls) + len(arrays)

        def body(*refs):
            kernel(*refs[:first], *refs[first + len(waits) :])

        results = pl.pallas_call(
            body,
            in_specs=[SM] * len(smalls) + [VM] * len(arrays) + [ANY] * len(waits),
            out_specs=[VM] * len(outs),
            out_shape=[jax.ShapeDtypeStruct(shape, dtype) for shape, dtype in outs],
            scratch_shapes=list(scratch),
            compiler_params=PARAMS,
            cost_estimate=cost,
            name=name,
        )(*smalls, *arrays, *waits)
        self.last = [results[last]]
        return results


def pause_kernel(o_ref):
    o_ref[...] = jnp.zeros_like(o_ref)


def pause(line, after=(), cost=LONG):
    line(pause_kernel, "pause", [((8, HD), F32)], [], [], after, (), cost)


def copy_kernel(*refs):
    outs = refs[len(refs) // 2 :]
    for ref, out in zip(refs, outs):
        out[...] = ref[...]


def merge_kernel(counts, *refs):
    first = 0
    for count, out in zip(counts, refs[sum(counts) :]):
        start = 0
        for ref in refs[first : first + count]:
            out[start : start + ref.shape[0]] = ref[...]
            start += ref.shape[0]
        first += count


def merged(line, groups):
    outs = [((sum(p.shape[0] for p in g), *g[0].shape[1:]), g[0].dtype) for g in groups]
    kernel = functools.partial(merge_kernel, [len(g) for g in groups])
    return line(kernel, "merge_inputs", outs, [], [p for g in groups for p in g])


def transpose_kernel(order, rows, at_ref, a_ref, near_ref, *refs):
    far_refs, flat = refs[:-1], refs[-1]
    flat[...] = a_ref[...].T.astype(flat.dtype)
    each = len(order) // len(far_refs)
    for yr in range(2):
        for dr in range(2):
            for i, low in enumerate(order):
                start = (((at_ref[2] ^ low) * 2 + (at_ref[0] ^ yr)) * 2 + (at_ref[1] ^ dr)) * rows
                piece = flat[pl.ds(pl.multiple_of(start, 8), rows), :].astype(BF)
                if yr == 0:
                    near_ref[i, dr] = piece
                else:
                    far_refs[i // each][i % each, dr] = piece


def transposed(line, at, a, order, rows):
    tokens, cols = a.shape
    halves = 2 if len(order) % 2 == 0 else 1
    outs = [((len(order), 2, rows, tokens), BF)] + [((len(order) // halves, 2, rows, tokens), BF)] * halves
    scratch = [pltpu.VMEM((cols, tokens), BF if rows % 16 == 0 else F32)]
    kernel = functools.partial(transpose_kernel, order, rows)
    return line(kernel, "transpose_inputs", outs, [at], [a], (), scratch)


def state_kernel(first, heads, flags_ref, ld_ref, q_ref, c_ref, pay_ref, own_ref, cum_ref, cumt_ref, qbf_ref):
    tokens = ld_ref.shape[1]
    half = (heads + 1) // 2
    y = flags_ref[0]
    x = ld_ref[first : first + heads, :]
    x = jnp.concatenate([x, jnp.zeros((PLANE - heads, tokens), F32)], axis=0)
    lane = lax.broadcasted_iota(jnp.int32, x.shape, 1)
    shift = 1
    while shift < tokens:
        x = x + jnp.where(lane >= shift, pltpu.roll(x, shift, 1), 0.0)
        shift *= 2
    cum_ref[...] = x
    xt = jnp.concatenate([x, jnp.zeros((HD - PLANE, tokens), F32)], axis=0).T
    cumt_ref[...] = xt
    et = jnp.exp(xt)
    d = jnp.broadcast_to(jnp.exp(x[:, tokens - 1 : tokens]), (PLANE, HD))
    later = jnp.concatenate([d[half:], d[:half]], axis=0)
    put_decays(jnp.where(y == 0, later, d), half, pay_ref, None)
    put_decays(jnp.where(y == 0, d, later), half, None, own_ref)

    def put_terms(low, high, at):
        s = slice(at * HD, (at + 1) * HD)
        own_ref[s, :] = jnp.where(y == 0, low, high)
        pay_ref[s, :] = jnp.where(y == 0, high, low).astype(BF)

    terms = []
    for h in range(heads):
        s = slice(h * HD, (h + 1) * HD)
        f = slice((first + h) * HD, (first + h + 1) * HD)
        q = q_ref[:, f].astype(F32).astype(BF)
        qbf_ref[:, s] = q
        hi, lo = hi_lo(c_ref[:, f].astype(F32) * et[:, h : h + 1])
        both = dot(q, jnp.concatenate([hi, lo], axis=1), ((0,), (0,)))
        terms.append(both[:, :HD] + both[:, HD:])
        if h >= half:
            put_terms(terms[h - half], terms[h], h - half)
    if heads % 2:
        put_terms(terms[half - 1], jnp.zeros((HD, HD), F32), half - 1)


def state_terms(line, first, heads, flags, q, c, ld):
    tokens = q.shape[0]
    rows = (heads + 1) // 2 * HD + EXTRA
    outs = [((rows, HD), BF), ((rows, HD), F32), ((PLANE, tokens), F32), ((tokens, HD), F32)]
    outs.append(((tokens, heads * HD), BF))
    return line(functools.partial(state_kernel, first, heads), "state_terms", outs, [flags], [ld, q, c])


def put_decays(d, heads, pay_ref, own_ref):
    at = heads * HD
    if pay_ref is not None:
        d_hi, d_mid = hi_lo(d)
        pay_ref[at : at + PLANE, :] = d_hi
        pay_ref[at + PLANE : at + 2 * PLANE, :] = d_mid
        pay_ref[at + 2 * PLANE : at + EXTRA, :] = (d - d_hi.astype(F32) - d_mid.astype(F32)).astype(BF)
    if own_ref is not None:
        own_ref[at : at + PLANE, :] = d
        own_ref[at + PLANE : at + EXTRA, :] = jnp.zeros((EXTRA - PLANE, HD), F32)


def decays(ref, heads):
    p = ref[heads * HD :, :].astype(F32)
    return p[:PLANE] + p[PLANE : 2 * PLANE] + p[2 * PLANE :]


def append_kernel(heads, at, flags_ref, a_ref, b_ref, pay_ref, own_ref):
    swap = flags_ref[at] != 0
    da, db = decays(a_ref, heads), decays(b_ref, heads)
    one = jnp.ones_like(da)
    scale_a = jnp.where(swap, db, one)
    scale_b = jnp.where(swap, one, da)
    put_decays(da * db, heads, pay_ref, own_ref)
    for h in range(heads):
        s = slice(h * HD, (h + 1) * HD)
        term = scale_a[h : h + 1] * a_ref[s, :].astype(F32) + scale_b[h : h + 1] * b_ref[s, :].astype(F32)
        own_ref[s, :] = term
        pay_ref[s, :] = term.astype(BF)


def append(line, heads, flags, at, a, b):
    outs = [(a.shape, BF), (a.shape, F32)]
    return line(functools.partial(append_kernel, heads, at), "join_states", outs, [flags], [a, b])


def local_kernel(heads, cols, q_ref, k_ref, c_ref, cum_ref, cumt_ref, o_ref, kbf_ref):
    tokens = q_ref.shape[0]
    tile = 256
    row = lax.broadcasted_iota(jnp.int32, (tile, tile), 0)
    col = lax.broadcasted_iota(jnp.int32, (tile, tile), 1)
    causal = col >= row
    for h in range(heads):
        f = slice(cols + h * HD, cols + (h + 1) * HD)
        k = k_ref[:, f].astype(F32).astype(BF)
        kbf_ref[:, h * HD : (h + 1) * HD] = k
        scores = dot(k, q_ref[:, h * HD : (h + 1) * HD], ((1,), (1,)))
        strips = []
        for at in range(0, tokens, tile):
            end = at + tile
            before = cumt_ref[at:end, h : h + 1]
            gap = jnp.where(causal, cum_ref[h : h + 1, at:end] - before, -jnp.inf)
            strip = [jnp.zeros((tile, at), BF)] if at else []
            strip.append((scores[at:end, at:end] * jnp.exp(gap)).astype(BF))
            if end < tokens:
                middle = cum_ref[h : h + 1, end - 1 : end]
                to_t = jnp.exp(cum_ref[h : h + 1, end:] - middle)
                from_s = jnp.exp(middle - before)
                strip.append((scores[at:end, end:] * to_t * from_s).astype(BF))
            strips.append(jnp.concatenate(strip, axis=1))
        weighted = jnp.concatenate(strips, axis=0)
        o_ref[:, h * HD : (h + 1) * HD] = dot(weighted, c_ref[:, f], ((1,), (0,)))


def local_part(line, first, heads, q, k, c, cum, cumt):
    kernel = functools.partial(local_kernel, heads, first * HD)
    shape = (q.shape[0], heads * HD)
    return line(kernel, "local_part", [(shape, F32), (shape, BF)], [], [q, k, c, cum, cumt])


def carry_kernel(heads, flags_ref, own_ref, oth_ref, e_ref, r_ref, theirs_ref, mine_ref):
    is_first = flags_ref[0] == 0
    de = decays(e_ref, heads)
    d_second = jnp.where(is_first, decays(oth_ref, heads), decays(own_ref, heads))
    for h in range(heads):
        s = slice(h * HD, (h + 1) * HD)
        second = e_ref[s, :].astype(F32) + de[h : h + 1] * r_ref[s, :].astype(F32)
        term = jnp.where(is_first, oth_ref[s, :].astype(F32), own_ref[s, :])
        first = term + d_second[h : h + 1] * second
        mine_ref[s, :] = jnp.where(is_first, first, second)
        theirs_ref[s, :] = jnp.where(is_first, second, first).astype(BF)


def carries(line, heads, flags, arrays):
    shape = (heads * HD, HD)
    kernel = functools.partial(carry_kernel, heads)
    return line(kernel, "carries", [(shape, BF), (shape, F32)], [flags], arrays)


def value_kernel(half, first, count, scale, flags_ref, k_ref, l_ref, cumt_ref, mine_ref, theirs_ref, o_ref):
    tokens = k_ref.shape[0]
    fall = jnp.exp(cumt_ref[tokens - 1 : tokens, :] - cumt_ref[...])
    for h in range(first, first + count):
        s = slice(h * HD, (h + 1) * HD)
        at = slice(h % half * HD, (h % half + 1) * HD)
        carry = jnp.where(flags_ref[0] == h // half, mine_ref[at, :], theirs_ref[at, :].astype(F32))
        hi, lo = hi_lo(carry)
        both = dot(k_ref[:, s], jnp.concatenate([hi, lo], axis=1), ((1,), (0,)))
        carried = fall[:, h : h + 1] * (both[:, :HD] + both[:, HD:])
        at = (h - first) * HD
        o_ref[:, at : at + HD] = (scale * (l_ref[:, s] + carried)).astype(BF)


def value_grads(line, half, first, count, scale, flags, arrays, after):
    kernel = functools.partial(value_kernel, half, first, count, scale)
    outs = [((arrays[0].shape[0], count * HD), BF)]
    return line(kernel, "value_grad", outs, [flags], arrays, after)[0]


def join_and_input_kernel(rows, at, flags_ref, *refs):
    *vs, w_ref, o_ref, v_all = refs
    start = 0
    for v in vs:
        v_all[:, start : start + v.shape[1]] = v[...]
        start += v.shape[1]
    input_kernel(rows, at, 0, flags_ref, v_all, w_ref, o_ref)


def input_kernel(rows, at, first, flags_ref, *refs):
    *before, v_ref, w_ref, o_ref = refs
    for done in before:
        o_ref[:, :first] = done[...]
    cols = o_ref.shape[1] - first
    w = w_ref[pl.ds(pl.multiple_of(flags_ref[at] * rows + first, 128), cols), :]
    o_ref[:, first:] = dot(v_ref[...], w, ((1,), (1,))).astype(o_ref.dtype)


def first_input_part(line, flags, at, vs, w, rows, dtype, end):
    tokens, features = vs[0].shape[0], w.shape[1]
    outs = [((tokens, end), dtype), ((tokens, features), BF)]
    kernel = functools.partial(join_and_input_kernel, rows, at)
    return line(kernel, "input_part", outs, [flags], [*vs, w])


def input_part(line, flags, at, v, w, rows, dtype, end, before=()):
    first = before[0].shape[1] if before else 0
    kernel = functools.partial(input_kernel, rows, at, first)
    return line(kernel, "input_part", [((v.shape[0], end), dtype)], [flags], [*before, v, w])[0]


def last_input_kernel(total_ref, *refs):
    total = total_ref[...]
    for ref in refs[:-2]:
        total = total + ref[...].astype(F32)
    refs[-2][...] = total.astype(BF)
    refs[-1][...] = jnp.zeros_like(refs[-1])


def last_weight_kernel(scale, *refs):
    out = refs[-1]
    start = 0
    for keep, came in zip(refs[0:-1:2], refs[1:-1:2]):
        width = keep.shape[2]
        out[:, start : start + width] = scale * (keep[0] + came[0].astype(F32))
        start += width


def weight_kernel(sides, *refs):
    *pieces, v_ref, v_y_ref, away_ref, keep_ref = refs
    for s in range(sides):
        own, other = pieces[2 * s : 2 * s + 2]
        lows, _, rows, tokens = own.shape
        total = dot(own[...].reshape(-1, tokens), v_ref[...], ((1,), (0,)))
        total = total + dot(other[...].reshape(-1, tokens), v_y_ref[...], ((1,), (0,)))
        for low in range(lows):
            at = low * 2 * rows
            keep_ref[low * sides + s] = total[at : at + rows]
            away_ref[low * sides + s] = total[at + rows : at + 2 * rows].astype(BF)


def weight_part(line, pieces, vs, after):
    sides, (lows, _, rows, _) = len(pieces), pieces[0][0].shape
    shape = (lows * sides, rows, vs[0].shape[1])
    arrays = [p for side_pieces in pieces for p in side_pieces] + list(vs)
    kernel = functools.partial(weight_kernel, sides)
    return line(kernel, "weight_part", [(shape, BF), (shape, F32)], [], arrays, after, last=1)


def fold_kernel(at, start, flags_ref, keep_ref, came_ref, away_ref, left_ref):
    half, _, width = away_ref.shape
    cols = slice(start, start + width)
    kept = pl.ds(flags_ref[at] * half, half)
    sent = pl.ds((1 - flags_ref[at]) * half, half)
    left_ref[...] = keep_ref[kept, :, cols] + came_ref[kept, :, cols].astype(F32)
    away_ref[...] = (keep_ref[sent, :, cols] + came_ref[sent, :, cols].astype(F32)).astype(BF)


def fold(line, flags, at, keep, came, start=0, width=None):
    blocks, rows, all_columns = keep.shape
    shape = (blocks // 2, rows, width or all_columns)
    kernel = functools.partial(fold_kernel, at, start)
    return line(kernel, "fold_weight", [(shape, BF), (shape, F32)], [flags], [keep, came])


def tied(x, *after):
    return lax.optimization_barrier((x, *after))[0]


def swap_with(x, axis, bit):
    return lax.ppermute(x, axis, [(i, i ^ bit) for i in range(lax.axis_size(axis))])


def from_later(x, axis, shift):
    return lax.ppermute(x, axis, [(i, i - shift) for i in range(shift, lax.axis_size(axis))])


def local(inputs, value_weight, cotangent, spikes_q, spikes_k, log_decay):
    seqs, sides, dps = lax.axis_size("seq"), lax.axis_size("head"), lax.axis_size("dp")
    seq, side, dp = lax.axis_index("seq"), lax.axis_index("head"), lax.axis_index("dp")
    y, z = seq % 2, seq // 2
    tokens, rows_here = inputs.shape[1:]
    features = value_weight.shape[1]
    heads_here = log_decay.shape[1]
    seq_length = tokens * seqs
    grad_scale = 1.0 / (2.25 * HD * math.sqrt(seq_length))
    third = (heads_here + 2) // 4
    splits = [(third - 1,) * 2, (third, heads_here - 3 * third + 2)] if heads_here > 8 else [(third, heads_here - third)]
    sizes = [sum(split) for split in splits]
    starts = [sum(sizes[:g]) for g in range(len(sizes))]
    groups = len(sizes)
    rows = rows_here * sides // (seqs * dps)
    lows = rows_here // (2 * dps * rows)
    stages = (seqs // 2).bit_length() - 1

    q, k, c, ld = spikes_q[0], spikes_k[0], cotangent[0], log_decay[0]

    low_bits = lows.bit_length() - 1
    order = [int("0" + format(i, "b").zfill(low_bits)[::-1], 2) for i in range(lows)] if low_bits else [0]
    here = (z // lows) ^ side
    bits = list(range(low_bits)) + list(reversed(range(low_bits, stages)))

    at_sides = 4
    at_steps = at_sides + sides
    places = [y, dp, z % lows, jnp.zeros_like(y)] + [side ^ i for i in range(sides)]
    places += [(here >> max(b - low_bits, 0)) & int(b >= low_bits) for b in bits]
    flags = jnp.stack([p.astype(jnp.int32) for p in places])

    line = Line()
    own, other, joined, locals_, carried, values, from_y = [], [], [], [], [], [], []
    halves = [(size + 1) // 2 for size in sizes]

    def states(g):
        own.append(state_terms(line, starts[g], sizes[g], flags, q, c, ld))
        other.append(swap_with(own[g][0], "seq", 1))

    def join(g):
        joined.append(append(line, halves[g], flags, 0, own[g][1], other[g]))

    def spread(g):
        pay, ours = joined[g]
        e = None
        for stage in range(stages):
            later = from_later(pay, "seq", 2 << stage)
            if stage == 0:
                e = later
            elif stage < stages - 1:
                e = append(line, halves[g], flags, 3, e, later)[1]
            if stage < stages - 1:
                pay, ours = append(line, halves[g], flags, 3, ours, later)
        if stages == 1:
            later = jnp.zeros_like(later)
        joined[g] = (e, later)

    def carry(g):
        theirs, mine = carries(line, halves[g], flags, [own[g][1], other[g], *joined[g]])
        carried.append((mine, swap_with(theirs, "seq", 1)))

    def local(g):
        _, _, cum, cumt, q_bf = own[g]
        locals_.append(local_part(line, starts[g], sizes[g], q_bf, k, c, cum, cumt))

    def value(g, *after):
        part, k_bf = locals_[g]
        arrays = [k_bf, part, own[g][3], *carried[g]]
        first = 0
        for count in splits[g]:
            v = value_grads(line, halves[g], first, count, grad_scale, flags, arrays, after)
            values.append(v)
            from_y.append(swap_with(v, "seq", 1))
            first, after = first + count, ()

    kept, parts = {}, {}

    def matmul(i, *after):
        away, keep = weight_part(line, pieces, (values[i], from_y[i]), after)
        parts[i] = (keep, swap_with(away, "dp", 1))

    def over_dp(i, j=0, start=0, width=None):
        away, keep = fold(line, flags, at_steps, *parts[i], start, width)
        kept[i, j] = (keep, swap_with(away, "seq", 2 << bits[0]))

    def over_z(i, j=0):
        for step, bit in enumerate(bits[1:], 1):
            away, keep = fold(line, flags, at_steps + step, *kept[i, j])
            kept[i, j] = (keep, swap_with(away, "seq", 2 << bit))

    others = []
    shares = (6, 9) if rows_here % (14 * HD) == 0 else (0, 0)

    def input_parts(at, dtype, step):
        middle = rows_here // 14 * shares[at != at_sides]
        common = (value_weight, rows_here, dtype)
        if step == 0 and not middle:
            return pause(line)
        if step == 0 and not all_values:
            part, v = first_input_part(line, flags, at, values, *common, middle)
            all_values.append(v)
            halves_done[at] = [part]
        elif step == 0:
            halves_done[at] = [input_part(line, flags, at, all_values[0], *common, middle)]
        elif not all_values:
            part, v = first_input_part(line, flags, at, values, *common, rows_here)
            all_values.append(v)
            return part
        else:
            return input_part(line, flags, at, all_values[0], *common, rows_here, halves_done.get(at, ()))

    all_values = []
    halves_done = {}

    def input_others(step):
        for i in range(1, sides):
            part = input_parts(at_sides + i, BF, step)
            if step:
                others.append(swap_with(part, "head", i))

    near, *far = transposed(line, flags, inputs[0], order, rows)
    near_x = [swap_with(near, "head", i) for i in range(1, sides)]
    for g in range(groups):
        states(g)
    far_x = [[] for _ in near_x]

    def send_far(i):
        piece = far[i]
        far[i] = swap_with(tied(piece, *line.last), "seq", 1)
        line.last.append(piece)

    def far_to_x(i):
        far[i] = line(copy_kernel, "pass_on", [(far[i].shape, BF)], [], [far[i]])[0]
        for j in range(1, sides):
            far_x[j - 1].append(swap_with(far[i], "head", j))

    send_far(0)
    join(0)
    if len(far) == 2:
        send_far(1)
    if groups == 2:
        join(1)
    local(0)
    spread(0)
    if groups == 2:
        local(1)
        spread(1)
    far_to_x(0)
    carry(0)
    if len(far) == 2:
        far_to_x(1)
    if groups == 2:
        carry(1)
    value(0, *near_x)
    if groups == 2:
        value(1, *[f[0] for f in far_x])
    everything = [[p] for p in (near, *near_x)] + [far, *far_x]
    everything = merged(line, everything)
    pieces = list(zip(everything[:sides], everything[sides:]))
    if groups == 2:
        matmul(0)
        input_others(0)
        over_dp(0)
        matmul(1)
        input_others(1)
        over_dp(1)
        over_z(0)
        matmul(2)
        input_parts(at_sides, F32, 0)
        over_dp(2)
        matmul(3)
        pause(line, [kept[0, 0][1]])
        over_z(1)
        over_dp(3, 0, 0, splits[1][1] // 2 * HD)
        over_dp(3, 1, splits[1][1] // 2 * HD, (splits[1][1] + 1) // 2 * HD)
        over_z(2)
        over_z(3, 0)
        over_z(3, 1)
        total = input_parts(at_sides, F32, 1)
    else:
        matmul(0)
        matmul(1)
        over_dp(0)
        over_dp(1)
        over_z(0)
        input_others(0)
        input_others(1)
        input_parts(at_sides, F32, 0)
        total = input_parts(at_sides, F32, 1)
        over_z(1)
    outs = [(total.shape, BF), ((8, HD), F32)]
    grad_input = line(last_input_kernel, "grad_input", outs, [], [total, *others], last=1)[0]
    arrays = [a for i in sorted(kept) for a in kept[i]]
    kernel = functools.partial(last_weight_kernel, 1.0 / math.sqrt(dps * seq_length))
    grad_weight = line(kernel, "grad_weight", [((rows, features), F32)], [], arrays)[0]
    return grad_input[None], grad_weight


def solution(mesh):
    return jax.shard_map(
        local,
        mesh=mesh,
        in_specs=(
            P("dp", "seq", "head"),
            P(None, "head"),
            P("dp", "seq", "head"),
            P("dp", "seq", "head"),
            P("dp", "seq", "head"),
            P("dp", "head", "seq"),
        ),
        out_specs=(P("dp", "seq", "head"), P(("seq", "dp"), "head")),
        check_vma=False,
    )
```
